512 devices in a mesh: fsdp: 64 (over y, x, core), tensor: 8 (over z).
Axes of the slice: x: 4, y: 8, z: 8, core: 2. Of those that a mesh axis runs over, the one named last changes fastest.
Arguments:
- momentum: float32 [7168, 28672], P('fsdp', 'tensor'), may hold values from -6 to 6
- gradient: bfloat16 [7168, 28672], P('fsdp', 'tensor'), may hold values from -40 to 40
- basis_panel: float32 [256, 28672], P('fsdp', 'tensor'), may hold values from -0.625 to 0.625
Outputs:
- momentum_new: float32 [7168, 28672], P('fsdp', 'tensor')
- basis_new: float32 [256, 28672], P('fsdp', 'tensor')
- update: bfloat16 [7168, 28672], P('fsdp', 'tensor')
The draws below stay inside these ranges and needn't reach their ends.
All inputs are finite; a program needn't handle non-finite values.
Results may differ from the reference program's by a relative error of at most 0.0012.
Values sent between devices are 32-bit elements; how exact they have to be, the bound alone decides.
No kernel may reach another device: no remote copies, remote signals or barrier semaphores. Data moves between devices by JAX's collectives and lax.ppermute only.
A program may use at most 64 MiB of HBM per device.

```python
import math
import jax
import jax.numpy as jnp
from jax import lax

ROWS = 7168
COLS = 28672
RANK = 256


def scale_profile(key, length):
    position = jnp.arange(length, dtype=jnp.float32) / length
    jitter = jax.random.uniform(key, (length,), jnp.float32)
    return jnp.exp(math.log(3.0) * position + math.log(10.0 / 3.0) * jitter)


def draw_gradient(key, part):
    key = jax.random.fold_in(key, 11)
    keys = jax.random.split(key, 3)
    row_scale = scale_profile(keys[0], ROWS)
    col_scale = scale_profile(keys[1], COLS)
    noise = jnp.clip(jax.random.normal(keys[2], (ROWS, COLS), jnp.float32), -4.0, 4.0)
    values = noise * row_scale[:, None] * col_scale[None, :] / 10.0
    return values.astype(jnp.bfloat16)


def draw_basis_panel(key, part):
    key = jax.random.fold_in(key, 23)
    keys = jax.random.split(key, 2)
    row_scale = scale_profile(keys[0], RANK)
    noise = jnp.clip(jax.random.normal(keys[1], (RANK, COLS), jnp.float32), -4.0, 4.0)
    return (noise * row_scale[:, None] / 64.0).astype(jnp.float32)


def levels(rng, dims, cuts, smallest, high):
    level, own = 1.0, jax.random.fold_in(rng, 6)
    for axis_at, blocks in cuts:
        steps = jnp.exp(jax.random.uniform(jax.random.fold_in(own, axis_at), (blocks,), jnp.float32, smallest / len(cuts), high / len(cuts)))
        level = level * jnp.repeat(steps, dims[axis_at] // blocks).reshape([-1 if axis == axis_at else 1 for axis in range(len(dims))])
    return level


def scatter_about(key, extent, deviation, most, shards=(), kind=jnp.bfloat16):
    drawn = jax.random.normal(key, extent, jnp.float32) * deviation
    if len(shards) > 0:
        drawn = levels(key, extent, shards, -0.22, 0.18) * drawn
    return jnp.clip(drawn, min=-most, max=most).astype(kind)


def setup_inputs(seed: int = 0) -> dict:
    key_of = jax.random.split(jax.random.key(seed), 4)
    momentum = scatter_about(key_of[0], (ROWS, COLS), 1.0, 6.0, ((0, 64), (1, 8)), jnp.float32)
    gradient = draw_gradient(jax.random.fold_in(key_of[3], 71), 0)
    basis_panel = draw_basis_panel(jax.random.fold_in(key_of[3], 71), 0)
    return {"momentum": momentum, "gradient": gradient, "basis_panel": basis_panel}


norm_eps = 1e-06
carry_keep = 0.9

def reference(momentum, gradient, basis_panel):
    highest = lax.Precision.HIGHEST
    combined = momentum + gradient.astype(jnp.float32)
    panel = lax.dot_general(combined, basis_panel, (((1,), (1,)), ((), ())), precision=highest, preferred_element_type=jnp.float32)
    panel_scale = jnp.sqrt(lax.optimization_barrier(jnp.sum(panel * panel, axis=0)) + norm_eps)
    left_panel = panel / panel_scale[None, :]
    right_panel = lax.dot_general(left_panel, combined, (((0,), (0,)), ((), ())), precision=highest, preferred_element_type=jnp.float32)
    right_scale = jnp.sqrt(lax.optimization_barrier(jnp.sum(right_panel * right_panel, axis=1)) + norm_eps)
    basis_new = right_panel / right_scale[:, None]
    momentum_new = combined - (1.0 - carry_keep) * jnp.dot(left_panel, right_panel, precision=highest, preferred_element_type=jnp.float32)
    update_scale = math.sqrt(ROWS * COLS / RANK)
    update = (update_scale * jnp.dot(left_panel, basis_new, precision=highest, preferred_element_type=jnp.float32)).astype(jnp.bfloat16)
    return (momentum_new, basis_new, update)
```

```python
import math

import jax
import jax.numpy as jnp
from jax import lax
from jax.sharding import Mesh, PartitionSpec as P

ROWS = 7168
COLS = 28672
RANK = 256

NY, NX, NC, NZ = 8, 4, 2, 8

norm_eps = 1e-06
carry_keep = 0.9
HIGH = lax.Precision.HIGH
SWAP = [(0, 1), (1, 0)]


def dot(a, b, dims):
    return lax.dot_general(
        a, b, (dims, ((), ())), precision=HIGH, preferred_element_type=jnp.float32
    )


def exchange(blocks, axes):
    return lax.all_to_all(blocks, axes, 0, 0, tiled=True)


def spread(block, axes, n):
    return exchange(jnp.broadcast_to(block[None], (n, *block.shape)), axes)


def shards(momentum, gradient, basis_panel):
    rows, cols = momentum.shape
    rank_rows = basis_panel.shape[0]
    part = cols // NX
    half = NY * NX * rank_rows
    own_ranks = NX * rank_rows
    padded = -(-rows // (8 * NZ)) * 8 * NZ
    chunk = padded // NZ
    combined = momentum + gradient.astype(jnp.float32)

    wide = combined.reshape(rows, NX, part).transpose(1, 0, 2)
    tall = exchange(wide, "x").reshape(NX * rows, part)
    pieces = basis_panel.reshape(rank_rows, NX, part).transpose(1, 0, 2)
    pieces = jnp.broadcast_to(pieces[None], (NY, NX, rank_rows, part))
    basis_own = exchange(pieces.reshape(NY * NX, rank_rows, part), ("y", "x"))
    basis_own = basis_own.reshape(half, part)
    basis_oth = lax.ppermute(basis_own, "core", SWAP)

    panel = jnp.concatenate(
        [dot(tall, basis_own, ((1,), (1,))), dot(tall, basis_oth, ((1,), (1,)))], axis=1
    )
    panel = panel.reshape(NX, rows, 2 * half)
    panel = jnp.pad(panel, ((0, 0), (0, padded - rows), (0, 0)))
    panel = exchange(panel.reshape(NX * NZ, chunk, 2 * half), ("x", "z"))
    panel = spread(jnp.sum(panel, axis=0), ("x", "z"), NX * NZ)
    panel = panel.reshape(NX, padded, 2 * half)[:, :rows]
    mine = lax.dynamic_index_in_dim(panel, lax.axis_index("x"), 0, keepdims=False)
    panel = panel.reshape(NX * rows, 2 * half)

    squares = jnp.sum(panel * panel, axis=0)

    def right(p, q):
        u = dot(p, tall, ((0,), (0,)))
        return jnp.concatenate([u, jnp.broadcast_to(q[:, None], (half, 128))], axis=1)

    right_oth = lax.ppermute(right(panel[:, half:], squares[half:]), "core", SWAP)
    right_sum = right(panel[:, :half], squares[:half]) + right_oth
    right_sum = exchange(right_sum.reshape(NY, own_ranks, part + 128), "y")
    right_sum = jnp.sum(right_sum, axis=0)
    square = right_sum[:, part : part + 1] + norm_eps
    scaled = right_sum[:, :part] / square
    sent = jnp.concatenate([scaled, jnp.broadcast_to(square, (own_ranks, 128))], axis=1)

    got = spread(sent, "y", NY).reshape(half, part + 128)
    scaled, square = got[:, :part], got[:, part]
    row_squares = square * jnp.sum(scaled * scaled, axis=1)
    row_squares = jnp.broadcast_to(row_squares[None, :], (8, half))
    row_squares = jnp.sum(spread(row_squares, ("x", "z"), NX * NZ), axis=0)[0]
    right_scale = jnp.sqrt(row_squares + norm_eps)
    scale_oth = lax.ppermute(right_scale, "core", SWAP)

    own = spread(scaled, "x", NX).transpose(1, 0, 2).reshape(half, cols)
    oth = lax.ppermute(own, "core", SWAP)
    at = lax.axis_index("y") * own_ranks + lax.axis_index("x") * rank_rows
    factor = jnp.sqrt(square) / right_scale
    basis_share = lax.dynamic_slice_in_dim(own, at, rank_rows, 0)
    basis_share = basis_share * lax.dynamic_slice_in_dim(factor, at, rank_rows, 0)[:, None]

    whole_scale = jnp.concatenate([right_scale, scale_oth])
    flat = ((1,), (0,))
    feedback = dot(mine[:, :half], own, flat) + dot(mine[:, half:], oth, flat)
    left = mine / whole_scale[None, :]
    update_sum = dot(left[:, :half], own, flat) + dot(left[:, half:], oth, flat)
    momentum_new = combined - (1.0 - carry_keep) * feedback
    update = (math.sqrt(ROWS * COLS / RANK) * update_sum).astype(jnp.bfloat16)
    return momentum_new, basis_share, update


def solution(mesh):
    fine = Mesh(mesh.devices.reshape(NY, NX, NC, NZ), ("y", "x", "core", "z"))
    spec = P(("y", "x", "core"), "z")
    return jax.shard_map(
        shards,
        mesh=fine,
        in_specs=(spec, spec, spec),
        out_specs=(spec, spec, spec),
        check_vma=False,
    )
```

```python
import functools
import math

import jax
import jax.numpy as jnp
from jax import lax
from jax.experimental import pallas as pl
from jax.experimental.pallas import tpu as pltpu
from jax.sharding import Mesh, PartitionSpec as P

ROWS = 7168
COLS = 28672
RANK = 256

NY, NX, NC, NZ = 8, 4, 2, 8

norm_eps = 1e-06
carry_keep = 0.9
SWAP = [(0, 1), (1, 0)]
PARAMS = pltpu.CompilerParams(vmem_limit_bytes=40 * 1024 * 1024)
SMEM = pl.BlockSpec(memory_space=pltpu.SMEM)


def split(value):
    high = value.astype(jnp.bfloat16)
    return high, (value - high.astype(jnp.float32)).astype(jnp.bfloat16)


def dot3(a, b, dims):
    dot = functools.partial(
        lax.dot_general, dimension_numbers=(dims, ((), ())), preferred_element_type=jnp.float32
    )
    return dot(a[1], b[0]) + dot(a[0], b[1]) + dot(a[0], b[0])


def cost(flops, nbytes):
    return pl.CostEstimate(flops=flops, bytes_accessed=nbytes, transcendentals=0)


def deal_kernel(x_ref, *refs):
    for m_ref, g_ref, o_ref in zip(refs[:NX], refs[NX : 2 * NX], refs[2 * NX :]):
        o_ref[...] = m_ref[...] + g_ref[...].astype(jnp.float32)


def deal(x, momentum, gradient):
    rows, cols = momentum.shape
    part = cols // NX
    block = [
        pl.BlockSpec((rows, part), lambda i, x_ref, j=j: (0, lax.rem(x_ref[0] + j, NX)))
        for j in range(NX)
    ]
    return pl.pallas_call(
        deal_kernel,
        grid_spec=pltpu.PrefetchScalarGridSpec(
            num_scalar_prefetch=1,
            grid=(1,),
            in_specs=block * 2,
            out_specs=[pl.BlockSpec((rows, part), lambda i, x_ref: (0, 0))] * NX,
        ),
        out_shape=[jax.ShapeDtypeStruct((rows, part), jnp.float32)] * NX,
        compiler_params=PARAMS,
        cost_estimate=cost(rows * cols, 10 * rows * cols),
    )(x, *[momentum] * NX, *[gradient] * NX)


def panel_kernel(x_ref, *refs):
    blocks, (own_ref, oth_ref, out_ref) = refs[:NX], refs[NX:]
    rows = blocks[0].shape[0]
    tall = split(jnp.concatenate([ref[...] for ref in blocks], axis=0))
    basis = split(jnp.concatenate([own_ref[...], oth_ref[...]], axis=0))
    panel = dot3(tall, basis, ((1,), (1,)))
    for j in range(NX):
        at = lax.rem(x_ref[0] + (NX - j), NX)
        out_ref[at, :rows] = panel[j * rows : (j + 1) * rows]
        if out_ref.shape[1] > rows:
            spare = (out_ref.shape[1] - rows, out_ref.shape[2])
            out_ref[at, rows:] = jnp.zeros(spare, jnp.float32)


def panel_part(x, blocks, own, oth, padded):
    rows, part = blocks[0].shape
    half = own.shape[0]
    return pl.pallas_call(
        panel_kernel,
        in_specs=[SMEM] + [pl.BlockSpec(memory_space=pltpu.VMEM)] * (NX + 2),
        out_specs=pl.BlockSpec(memory_space=pltpu.VMEM),
        out_shape=jax.ShapeDtypeStruct((NX, padded, 2 * half), jnp.float32),
        compiler_params=PARAMS,
        cost_estimate=cost(12 * NX * rows * part * half, 4 * (NX * rows + 2 * half) * part),
    )(x, *blocks, own, oth)


def right_kernel(side, x_ref, *refs):
    blocks, (panel_ref, out_ref) = refs[:NX], refs[NX:]
    rows, half = blocks[0].shape[0], out_ref.shape[0]
    tall = split(jnp.concatenate([ref[...] for ref in blocks], axis=0))
    panel = [
        panel_ref[lax.rem(x_ref[0] + (NX - j), NX), :rows, side * half : (side + 1) * half]
        for j in range(NX)
    ]
    out_ref[...] = dot3(split(jnp.concatenate(panel, axis=0)), tall, ((0,), (0,)))


def right_part(side, x, blocks, panel):
    rows, part = blocks[0].shape
    half = panel.shape[2] // 2
    return pl.pallas_call(
        functools.partial(right_kernel, side),
        in_specs=[SMEM] + [pl.BlockSpec(memory_space=pltpu.VMEM)] * (NX + 1),
        out_specs=pl.BlockSpec(memory_space=pltpu.VMEM),
        out_shape=jax.ShapeDtypeStruct((half, part), jnp.float32),
        compiler_params=PARAMS,
        cost_estimate=cost(6 * NX * rows * part * half, 4 * NX * rows * part),
    )(x, *blocks, panel)


def low_rank(panel_ref, x, rows, factor, own_ref, oth_ref):
    left = panel_ref[x, :rows] * jnp.concatenate([factor[:1], factor[1:2]], axis=1)
    whole = jnp.concatenate([own_ref[0], oth_ref[0]], axis=0)
    return dot3(split(left), split(whole), ((1,), (0,)))


def momentum_kernel(at_ref, panel_ref, square_ref, m_ref, g_ref, own_ref, oth_ref, out_ref):
    factor = (1.0 - carry_keep) / square_ref[...]
    feedback = low_rank(panel_ref, at_ref[0], m_ref.shape[0], factor, own_ref, oth_ref)
    out_ref[...] = m_ref[...] + g_ref[...].astype(jnp.float32) - feedback


def momentum_out(at, panel, square, momentum, gradient, own, oth):
    rows, cols = momentum.shape
    half, part = own.shape[1:]
    block = pl.BlockSpec((rows, part), lambda j: (0, j))
    right = pl.BlockSpec((1, half, part), lambda j: (j, 0, 0))
    return pl.pallas_call(
        momentum_kernel,
        grid=(NX,),
        in_specs=[
            SMEM,
            pl.BlockSpec(panel.shape, lambda j: (0, 0, 0)),
            pl.BlockSpec(square.shape, lambda j: (0, 0)),
            block,
            block,
            right,
            right,
        ],
        out_specs=block,
        out_shape=jax.ShapeDtypeStruct((rows, cols), jnp.float32),
        compiler_params=PARAMS,
        cost_estimate=cost(12 * rows * cols * half, 4 * (3 * rows + 2 * half) * cols),
    )(at, panel, square, momentum, gradient, own, oth)


def update_kernel(at_ref, panel_ref, square_ref, sums_ref, own_ref, oth_ref, out_ref, basis_ref):
    square = square_ref[...]
    right_scale = jnp.sqrt(sums_ref[...] / square + norm_eps)
    factor = math.sqrt(ROWS * COLS / RANK) / (square * right_scale)
    rows, (ranks, _) = out_ref.shape[0], basis_ref.shape
    update = low_rank(panel_ref, at_ref[0], rows, factor, own_ref, oth_ref)
    out_ref[...] = update.astype(jnp.bfloat16)
    first = at_ref[1]
    group = pl.multiple_of(first // 8 * 8, 8)
    eight = own_ref[0, pl.ds(group, 8), :]
    lane = lax.broadcasted_iota(jnp.int32, (8, square.shape[1]), 1)
    row = lax.broadcasted_iota(jnp.int32, (8, square.shape[1]), 0)
    scale = 1.0 / (jnp.sqrt(square[:1]) * right_scale[:1])
    scale = jnp.sum(jnp.where(lane == row + group, scale, 0.0), axis=1, keepdims=True)
    eight = eight * scale
    basis_ref[...] = jnp.where(first > group, eight[8 - ranks :], eight[:ranks])


def update_out(at, panel, square, sums, own, oth, rows, ranks):
    half, part = own.shape[1:]
    cols = NX * part
    right = pl.BlockSpec((1, half, part), lambda j: (j, 0, 0))
    small = pl.BlockSpec(square.shape, lambda j: (0, 0))
    return pl.pallas_call(
        update_kernel,
        grid=(NX,),
        in_specs=[SMEM, pl.BlockSpec(panel.shape, lambda j: (0, 0, 0)), small, small, right, right],
        out_specs=[
            pl.BlockSpec((rows, part), lambda j: (0, j)),
            pl.BlockSpec((ranks, part), lambda j: (0, j)),
        ],
        out_shape=[
            jax.ShapeDtypeStruct((rows, cols), jnp.bfloat16),
            jax.ShapeDtypeStruct((ranks, cols), jnp.float32),
        ],
        compiler_params=PARAMS,
        cost_estimate=cost(12 * rows * cols * half, 4 * (rows + 2 * half) * cols),
    )(at, panel, square, sums, own, oth)


def exchange(blocks, axes):
    return lax.all_to_all(blocks, axes, 0, 0, tiled=True)


def spread(block, axes, n):
    return exchange(jnp.broadcast_to(block[None], (n, *block.shape)), axes)


def shards(momentum, gradient, basis_panel):
    rows, cols = momentum.shape
    rank_rows = basis_panel.shape[0]
    part = cols // NX
    half = NY * NX * rank_rows
    own_ranks = NX * rank_rows
    padded = -(-rows // (8 * NZ)) * 8 * NZ
    x, core = lax.axis_index("x"), lax.axis_index("core")
    at = jnp.stack([x, lax.axis_index("y") * own_ranks + x * rank_rows]).astype(jnp.int32)

    pieces = basis_panel.reshape(rank_rows, NX, part).transpose(1, 0, 2)
    pieces = jnp.broadcast_to(pieces[None], (NY, NX, rank_rows, part))
    basis_own = exchange(pieces.reshape(NY * NX, rank_rows, part), ("y", "x"))
    blocks = deal(at, momentum, gradient)
    blocks = [blocks[0]] + [
        lax.ppermute(blocks[j], "x", [(i, (i + j) % NX) for i in range(NX)]) for j in range(1, NX)
    ]
    basis_own = basis_own.reshape(half, part)
    basis_oth = lax.ppermute(basis_own, "core", SWAP)

    panel = panel_part(at, blocks, basis_own, basis_oth, padded)
    panel = exchange(panel.reshape(NX * NZ, padded // NZ, 2 * half), ("x", "z"))
    panel = spread(jnp.sum(panel, axis=0), ("x", "z"), NX * NZ)
    panel = panel.reshape(NX, padded, 2 * half)

    right_oth = lax.ppermute(right_part(1, at, blocks, panel), "core", SWAP)
    right_sum = right_part(0, at, blocks, panel) + right_oth
    right_sum = jnp.sum(exchange(right_sum.reshape(NY, own_ranks, part), "y"), axis=0)

    square = jnp.sum(panel * panel, axis=(0, 1)).reshape(2, half)
    beside = jnp.zeros((own_ranks, 128), jnp.float32).at[:2, :half].set(square)
    got = spread(jnp.concatenate([right_sum, beside], axis=1), "y", NY)
    square = jnp.sum(got[:, :2, part : part + half], axis=0)
    square = square + lax.ppermute(square, "core", SWAP)[::-1] + norm_eps

    own = spread(got[:, :, :part].reshape(half, part), "x", NX)
    oth = lax.ppermute(own, "core", SWAP)
    sums = jnp.broadcast_to(jnp.sum(own * own, axis=(0, 2)), (8, half))
    sums = jnp.sum(spread(sums, ("core", "z"), NC * NZ).reshape(NC, NZ, 8, half), axis=1)[:, 0]
    sums = jnp.where(core == 0, sums, sums[::-1])

    momentum_new = momentum_out(at, panel, square, momentum, gradient, own, oth)
    update, basis_new = update_out(at, panel, square, sums, own, oth, rows, rank_rows)
    return momentum_new, basis_new, update


def solution(mesh):
    fine = Mesh(mesh.devices.reshape(NY, NX, NC, NZ), ("y", "x", "core", "z"))
    spec = P(("y", "x", "core"), "z")
    return jax.shard_map(
        shards,
        mesh=fine,
        in_specs=(spec, spec, spec),
        out_specs=(spec, spec, spec),
        check_vma=False,
    )
```

```python
import functools
import math

import jax
import jax.numpy as jnp
from jax import lax
from jax.experimental import pallas as pl
from jax.experimental.pallas import tpu as pltpu
from jax.sharding import Mesh, PartitionSpec as P

ROWS = 7168
COLS = 28672
RANK = 256

NY, NX, NC, NZ = 8, 4, 2, 8

norm_eps = 1e-06
carry_keep = 0.9
SWAP = [(0, 1), (1, 0)]
PARAMS = pltpu.CompilerParams(vmem_limit_bytes=10 * 1024 * 1024)
VMEM = pl.BlockSpec(memory_space=pltpu.VMEM)
ANY = pl.BlockSpec(memory_space=pl.ANY)


def split(value):
    high = value.astype(jnp.bfloat16)
    return high, (value - high.astype(jnp.float32)).astype(jnp.bfloat16)


def dot3(a, b, dims):
    dot = functools.partial(
        lax.dot_general, dimension_numbers=(dims, ((), ())), preferred_element_type=jnp.float32
    )
    return dot(a[1], b[0]) + dot(a[0], b[1]) + dot(a[0], b[0])


def cost(flops, nbytes):
    return pl.CostEstimate(flops=flops, bytes_accessed=nbytes, transcendentals=0)


def deal_kernel(m_ref, g_ref, basis_ref, *refs):
    blocks, pieces_ref = refs[:NX], refs[NX]
    part = blocks[0].shape[1]
    for j, ref in enumerate(blocks):
        at = lax.rem(lax.axis_index("x") + j, NX)
        columns = pl.ds(pl.multiple_of(at * part, 128), part)
        ref[...] = m_ref[:, columns] + g_ref[:, columns].astype(jnp.float32)
    for to in range(NX):
        piece = basis_ref[:, to * part : (to + 1) * part]
        for y in range(NY):
            pieces_ref[y * NX + to] = piece


def deal(momentum, gradient, basis):
    rows, cols = momentum.shape
    ranks, part = basis.shape[0], cols // NX
    shapes = [(rows, part)] * NX + [(NY * NX, ranks, part)]
    return pl.pallas_call(
        deal_kernel,
        in_specs=[VMEM] * 3,
        out_specs=[VMEM] * (NX + 1),
        out_shape=[jax.ShapeDtypeStruct(shape, jnp.float32) for shape in shapes],
        compiler_params=PARAMS,
        cost_estimate=cost(rows * cols, 10 * rows * cols),
    )(momentum, gradient, basis)


def tall_kernel(*refs):
    blocks, (high_ref, low_ref) = refs[:NX], refs[NX:]
    rows = blocks[0].shape[0]
    for j, ref in enumerate(blocks):
        at = slice(j * rows, (j + 1) * rows)
        high_ref[at], low_ref[at] = split(ref[...])


def tall_parts(blocks):
    rows, part = blocks[0].shape
    shape = jax.ShapeDtypeStruct((NX * rows, part), jnp.bfloat16)
    return pl.pallas_call(
        tall_kernel,
        in_specs=[VMEM] * NX,
        out_specs=[VMEM] * 2,
        out_shape=[shape] * 2,
        compiler_params=PARAMS,
        cost_estimate=cost(4 * NX * rows * part, 8 * NX * rows * part),
    )(*blocks)


def panel_kernel(high_ref, low_ref, own_ref, oth_ref, out_ref):
    rows = high_ref.shape[0] // NX
    basis = split(jnp.concatenate([own_ref[...], oth_ref[...]], axis=0))
    panel = dot3((high_ref[...], low_ref[...]), basis, ((1,), (1,)))
    for j in range(NX):
        at = lax.rem(lax.axis_index("x") + (NX - j), NX)
        out_ref[at, :rows] = panel[j * rows : (j + 1) * rows]
        if out_ref.shape[1] > rows:
            spare = (out_ref.shape[1] - rows, out_ref.shape[2])
            out_ref[at, rows:] = jnp.zeros(spare, jnp.float32)


def panel_part(tall, own, oth, padded):
    rows, part = tall[0].shape
    half = own.shape[0]
    return pl.pallas_call(
        panel_kernel,
        in_specs=[VMEM] * 4,
        out_specs=VMEM,
        out_shape=jax.ShapeDtypeStruct((NX, padded, 2 * half), jnp.float32),
        compiler_params=PARAMS,
        cost_estimate=cost(12 * rows * part * half, 4 * (rows + 2 * half) * part),
    )(*tall, own, oth)


def right_kernel(side, high_ref, low_ref, panel_ref, out_ref, mine_ref=None):
    rows, half = high_ref.shape[0] // NX, panel_ref.shape[2] // 2
    tall = (high_ref[...], low_ref[...])
    panel = [panel_ref[lax.rem(lax.axis_index("x") + (NX - j), NX), :rows] for j in range(NX)]
    if side == 0:
        mine_ref[...] = panel[0]
    panel = jnp.concatenate(panel, axis=0)
    out_ref[half:] = jnp.zeros((8, out_ref.shape[1]), jnp.float32)
    squares = jnp.sum(panel * panel, axis=0, keepdims=True)
    out_ref[half : half + 1, :half] = squares[:, side * half : (side + 1) * half]
    out_ref[half : half + 1, half : 2 * half] = squares[:, (1 - side) * half : (2 - side) * half]
    panel = panel[:, side * half : (side + 1) * half]
    out_ref[:half] = dot3(split(panel), tall, ((0,), (0,)))


def right_part(side, tall, panel):
    rows, part = tall[0].shape
    half = panel.shape[2] // 2
    shapes = [(half + 8, part), (rows // NX, 2 * half)][: 2 - side]
    return pl.pallas_call(
        functools.partial(right_kernel, side),
        in_specs=[VMEM] * 3,
        out_specs=[VMEM] * len(shapes),
        out_shape=[jax.ShapeDtypeStruct(shape, jnp.float32) for shape in shapes],
        compiler_params=PARAMS,
        cost_estimate=cost(6 * rows * part * half, 4 * rows * part),
    )(*tall, panel)


def first_kernel(mine_ref, square_ref, m_ref, g_ref, own_ref, out_ref):
    half = own_ref.shape[1]
    left = mine_ref[:, :half] * ((1.0 - carry_keep) / square_ref[:1])
    feedback = dot3(split(left), split(own_ref[0]), ((1,), (0,)))
    out_ref[...] = m_ref[...] + g_ref[...].astype(jnp.float32) - feedback


def first_out(mine, square, momentum, gradient, own):
    rows, cols = momentum.shape
    half, part = own.shape[1:]
    block = pl.BlockSpec((rows, part), lambda j: (0, j))
    return pl.pallas_call(
        first_kernel,
        grid=(NX,),
        in_specs=[
            pl.BlockSpec(mine.shape, lambda j: (0, 0)),
            pl.BlockSpec(square.shape, lambda j: (0, 0)),
            block,
            block,
            pl.BlockSpec((1, half, part), lambda j: (j, 0, 0)),
        ],
        out_specs=block,
        out_shape=jax.ShapeDtypeStruct((rows, cols), jnp.float32),
        compiler_params=PARAMS,
        cost_estimate=cost(6 * rows * cols * half, 4 * (3 * rows + half) * cols),
    )(mine, square, momentum, gradient, own)


def stack(*arrays):
    return jnp.concatenate(arrays, axis=0)


def last_kernel(
    mine_ref, square_ref, sums_ref, own_ref, oth_ref, first_ref,
    m_out, u_out, b_out, m_buf, u_buf, b_buf, sems,
):
    rows, (ranks, _) = mine_ref.shape[0], b_buf.shape
    half, part = own_ref.shape[1:]
    loads = []
    for j in range(NX):
        at = (slice(None), pl.ds(j * part, part))
        loads.append(pltpu.make_async_copy(first_ref.at[at], m_buf.at[at], sems.at[j, 2]))
        loads[-1].start()
    square = square_ref[...]
    right_scale = jnp.sqrt(sums_ref[...] / square + norm_eps)
    for_update = math.sqrt(ROWS * COLS / RANK) / (square * right_scale)
    m_oth = split(mine_ref[:, half:] * ((1.0 - carry_keep) / square[1:2]))
    u_oth = split(mine_ref[:, half:] * for_update[1:2])
    u_own = split(mine_ref[:, :half] * for_update[:1])
    first = (lax.axis_index("y") * NX + lax.axis_index("x")) * ranks
    group = pl.multiple_of(first // 8 * 8, 8)
    lane = lax.broadcasted_iota(jnp.int32, (8, half), 1)
    row = lax.broadcasted_iota(jnp.int32, (8, half), 0)
    scale = 1.0 / (jnp.sqrt(square[:1]) * right_scale[:1])
    scale = jnp.sum(jnp.where(lane == row + group, scale, 0.0), axis=1, keepdims=True)

    dot = functools.partial(jnp.dot, preferred_element_type=jnp.float32)
    copies = []
    for j in range(NX):
        columns = pl.ds(j * part, part)
        high, low = split(oth_ref[j])
        sums = dot(stack(*m_oth, *u_oth), high)
        rest = dot(stack(m_oth[0], u_oth[0]), low)
        feedback = sums[:rows] + sums[rows : 2 * rows] + rest[:rows]
        update = sums[2 * rows : 3 * rows] + sums[3 * rows :] + rest[rows:]
        high, low = split(own_ref[j])
        sums = dot(stack(*u_own), high)
        update += sums[:rows] + sums[rows:] + dot(u_own[0], low)
        loads[j].wait()
        m_buf[:, columns] -= feedback
        u_buf[:, columns] = update.astype(jnp.bfloat16)
        eight = own_ref[j, pl.ds(group, 8), :] * scale
        b_buf[:, columns] = jnp.where(first > group, eight[8 - ranks :], eight[:ranks])
        for i, (buf, out) in enumerate(((m_buf, m_out), (u_buf, u_out))):
            at = (slice(None), columns)
            copies.append(pltpu.make_async_copy(buf.at[at], out.at[at], sems.at[j, i]))
            copies[-1].start()
    copies.append(pltpu.make_async_copy(b_buf, b_out, sems.at[NX, 0]))
    copies[-1].start()
    for copy in copies:
        copy.wait()


def last_out(mine, square, sums, own, oth, first, ranks):
    rows, cols = first.shape
    half = own.shape[1]
    shapes = [
        ((rows, cols), jnp.float32),
        ((rows, cols), jnp.bfloat16),
        ((ranks, cols), jnp.float32),
    ]
    return pl.pallas_call(
        last_kernel,
        in_specs=[VMEM] * 5 + [ANY],
        out_specs=[ANY] * 3,
        out_shape=[jax.ShapeDtypeStruct(*shape) for shape in shapes],
        scratch_shapes=[pltpu.VMEM(*shape) for shape in shapes]
        + [pltpu.SemaphoreType.DMA((NX + 1, 3))],
        compiler_params=PARAMS,
        cost_estimate=cost(18 * rows * cols * half, 4 * (4 * rows + 2 * half) * cols),
    )(mine, square, sums, own, oth, first)


def exchange(blocks, axes):
    return lax.all_to_all(blocks, axes, 0, 0, tiled=True)


def spread(block, axes, n):
    return exchange(jnp.broadcast_to(block[None], (n, *block.shape)), axes)


def shards(momentum, gradient, basis_panel):
    rows, cols = momentum.shape
    rank_rows = basis_panel.shape[0]
    part = cols // NX
    half = NY * NX * rank_rows
    own_ranks = NX * rank_rows
    padded = -(-rows // (8 * NZ)) * 8 * NZ
    core = lax.axis_index("core")

    *blocks, pieces = deal(momentum, gradient, basis_panel)
    blocks = [blocks[0]] + [
        lax.ppermute(blocks[j], "x", [(i, (i + j) % NX) for i in range(NX)]) for j in range(1, NX)
    ]
    basis_own = exchange(pieces, ("y", "x"))
    basis_own, *blocks = lax.optimization_barrier((basis_own, *blocks))
    basis_own = basis_own.reshape(half, part)
    basis_oth = lax.ppermute(basis_own, "core", SWAP)

    tall = tall_parts(blocks)
    panel = panel_part(tall, basis_own, basis_oth, padded)
    panel = exchange(panel.reshape(NX * NZ, padded // NZ, 2 * half), ("x", "z"))
    panel = spread(jnp.sum(panel, axis=0), ("x", "z"), NX * NZ)
    panel = panel.reshape(NX, padded, 2 * half)

    right_oth = lax.ppermute(right_part(1, tall, panel)[0], "core", SWAP)
    right_sum, mine = right_part(0, tall, panel)
    right_sum = right_sum + right_oth
    square = right_sum[half, : 2 * half].reshape(2, half)
    right_sum = exchange(right_sum[:half].reshape(NY, own_ranks, part), "y")
    right_sum = jnp.sum(right_sum, axis=0)
    beside = jnp.zeros((own_ranks, 128), jnp.float32).at[:2, :half].set(square)
    got = spread(jnp.concatenate([right_sum, beside], axis=1), "y", NY)
    square = jnp.sum(got[:, :2, part : part + half], axis=0) + norm_eps

    own = spread(got[:, :, :part].reshape(half, part), "x", NX)
    oth = lax.ppermute(own, "core", SWAP)
    sums = jnp.broadcast_to(jnp.sum(own * own, axis=(0, 2)), (8, half))
    sums = jnp.sum(spread(sums, ("core", "z"), NC * NZ).reshape(NC, NZ, 8, half), axis=1)[:, 0]
    sums = jnp.where(core == 0, sums, sums[::-1])

    first = first_out(mine, square, momentum, gradient, own)
    momentum_new, update, basis_new = last_out(mine, square, sums, own, oth, first, rank_rows)
    return momentum_new, basis_new, update


def solution(mesh):
    fine = Mesh(mesh.devices.reshape(NY, NX, NC, NZ), ("y", "x", "core", "z"))
    spec = P(("y", "x", "core"), "z")
    return jax.shard_map(
        shards,
        mesh=fine,
        in_specs=(spec, spec, spec),
        out_specs=(spec, spec, spec),
        check_vma=False,
    )
```

```python
import functools
import math

import jax
import jax.numpy as jnp
from jax import lax
from jax.experimental import pallas as pl
from jax.experimental.pallas import tpu as pltpu
from jax.sharding import Mesh, PartitionSpec as P

ROWS = 7168
COLS = 28672
RANK = 256

NY, NX, NC, NZ = 8, 4, 2, 8

norm_eps = 1e-06
carry_keep = 0.9
SWAP = [(0, 1), (1, 0)]
PARAMS = pltpu.CompilerParams(vmem_limit_bytes=10 * 1024 * 1024)
VMEM = pl.BlockSpec(memory_space=pltpu.VMEM)
ANY = pl.BlockSpec(memory_space=pl.ANY)
HBM = pl.BlockSpec(memory_space=pltpu.HBM)


def split(value):
    high = value.astype(jnp.bfloat16)
    return high, (value - high.astype(jnp.float32)).astype(jnp.bfloat16)


def dot3(a, b, dims):
    dot = functools.partial(
        lax.dot_general, dimension_numbers=(dims, ((), ())), preferred_element_type=jnp.float32
    )
    return dot(a[1], b[0]) + dot(a[0], b[1]) + dot(a[0], b[0])


def cost(flops, nbytes):
    return pl.CostEstimate(flops=flops, bytes_accessed=nbytes, transcendentals=0)


def deal_kernel(m_ref, g_ref, *refs):
    blocks, (m_buf, g_buf, sems) = refs[:NX], refs[NX:]
    part = blocks[0].shape[1]
    loads = []
    for j in range(NX):
        at = lax.rem(lax.axis_index("x") + j, NX)
        columns = (slice(None), pl.ds(pl.multiple_of(at * part, 128), part))
        loads.append(
            (
                pltpu.make_async_copy(m_ref.at[columns], m_buf.at[j], sems.at[j, 0]),
                pltpu.make_async_copy(g_ref.at[columns], g_buf.at[j], sems.at[j, 1]),
            )
        )
    for j in (*range(1, NX), 0):
        for load in loads[j]:
            load.start()
    for j in (*range(1, NX), 0):
        for load in loads[j]:
            load.wait()
        blocks[j][...] = m_buf[j] + g_buf[j].astype(jnp.float32)


def deal(momentum, gradient):
    rows, cols = momentum.shape
    part = cols // NX
    return pl.pallas_call(
        deal_kernel,
        in_specs=[HBM] * 2,
        out_specs=[VMEM] * NX,
        out_shape=[jax.ShapeDtypeStruct((rows, part), jnp.float32)] * NX,
        scratch_shapes=[
            pltpu.VMEM((NX, rows, part), jnp.float32),
            pltpu.VMEM((NX, rows, part), jnp.bfloat16),
            pltpu.SemaphoreType.DMA((NX, 2)),
        ],
        compiler_params=PARAMS,
        cost_estimate=cost(rows * cols, 10 * rows * cols),
    )(momentum, gradient)


def pieces_kernel(basis_ref, after_ref, pieces_ref):
    part = pieces_ref.shape[2]
    for to in range(NX):
        piece = basis_ref[:, to * part : (to + 1) * part]
        for y in range(NY):
            pieces_ref[y * NX + to] = piece


def basis_pieces(basis, after):
    ranks, cols = basis.shape
    pieces = (NY * NX, ranks, cols // NX)
    return pl.pallas_call(
        pieces_kernel,
        in_specs=[VMEM, ANY],
        out_specs=VMEM,
        out_shape=jax.ShapeDtypeStruct(pieces, jnp.float32),
        compiler_params=PARAMS,
        cost_estimate=cost(10**10, 10**8),
    )(basis, after)


def tall_kernel(*refs):
    blocks, (high_ref, low_ref) = refs[:NX], refs[NX:]
    rows = blocks[0].shape[0]
    for j, ref in enumerate(blocks):
        at = slice(j * rows, (j + 1) * rows)
        high_ref[at], low_ref[at] = split(ref[...])


def tall_parts(blocks):
    rows, part = blocks[0].shape
    shape = jax.ShapeDtypeStruct((NX * rows, part), jnp.bfloat16)
    return pl.pallas_call(
        tall_kernel,
        in_specs=[VMEM] * NX,
        out_specs=[VMEM] * 2,
        out_shape=[shape] * 2,
        compiler_params=PARAMS,
        cost_estimate=cost(10**10, 2 * 10**8),
    )(*blocks)


def panel_kernel(high_ref, low_ref, basis_ref, out_ref):
    rows = high_ref.shape[0] // NX
    panel = dot3((high_ref[...], low_ref[...]), split(basis_ref[...]), ((1,), (1,)))
    for j in range(NX):
        at = lax.rem(lax.axis_index("x") + (NX - j), NX)
        out_ref[at, :rows] = panel[j * rows : (j + 1) * rows]
        if out_ref.shape[1] > rows:
            spare = (out_ref.shape[1] - rows, out_ref.shape[2])
            out_ref[at, rows:] = jnp.zeros(spare, jnp.float32)


def panel_part(tall, basis, padded):
    rows, part = tall[0].shape
    half = basis.shape[0]
    return pl.pallas_call(
        panel_kernel,
        in_specs=[VMEM] * 3,
        out_specs=VMEM,
        out_shape=jax.ShapeDtypeStruct((NX, padded, half), jnp.float32),
        compiler_params=PARAMS,
        cost_estimate=cost(6 * rows * part * half, 4 * (rows + half) * part),
    )(*tall, basis)


def right_kernel(side, high_ref, low_ref, panel_ref, out_ref, mine_ref=None):
    rows, half = high_ref.shape[0] // NX, panel_ref.shape[2] // 2
    tall = (high_ref[...], low_ref[...])
    panel = [panel_ref[lax.rem(lax.axis_index("x") + (NX - j), NX), :rows] for j in range(NX)]
    if side == 0:
        mine_ref[...] = panel[0]
    panel = jnp.concatenate(panel, axis=0)
    out_ref[half:] = jnp.zeros((8, out_ref.shape[1]), jnp.float32)
    squares = jnp.sum(panel * panel, axis=0, keepdims=True)
    out_ref[half : half + 1, :half] = squares[:, side * half : (side + 1) * half]
    out_ref[half : half + 1, half : 2 * half] = squares[:, (1 - side) * half : (2 - side) * half]
    panel = panel[:, side * half : (side + 1) * half]
    out_ref[:half] = dot3(split(panel), tall, ((0,), (0,)))


def right_part(side, tall, panel):
    rows, part = tall[0].shape
    half = panel.shape[2] // 2
    shapes = [(half + 8, part), (rows // NX, 2 * half)][: 2 - side]
    return pl.pallas_call(
        functools.partial(right_kernel, side),
        in_specs=[VMEM] * 3,
        out_specs=[VMEM] * len(shapes),
        out_shape=[jax.ShapeDtypeStruct(shape, jnp.float32) for shape in shapes],
        compiler_params=PARAMS,
        cost_estimate=cost(6 * rows * part * half, 4 * rows * part),
    )(*tall, panel)


def product(left, own_ref, oth_ref, at=0):
    rows = left.shape[0] // 2
    high, low = split(jnp.concatenate([own_ref[at], oth_ref[at]], axis=0))
    dot = functools.partial(jnp.dot, preferred_element_type=jnp.float32)
    sums = dot(left, high)
    return sums[:rows] + sums[rows:] + dot(left[:rows], low)


def scaled(mine_ref, factor):
    return jnp.concatenate(split(mine_ref[...] * factor), axis=0)


def row(pair):
    return jnp.concatenate([pair[:1], pair[1:2]], axis=1)


def squares_kernel(own_ref, oth_ref, out_ref):
    nz, lines, _ = out_ref.shape
    part = own_ref.shape[2]
    ones = jnp.ones((lines, part), jnp.bfloat16)
    total = 0.0
    for j in range(NX):
        block = jnp.concatenate([own_ref[j], oth_ref[j]], axis=0)
        for piece in split(block * block):
            dims = (((1,), (1,)), ((), ()))
            total += lax.dot_general(ones, piece, dims, preferred_element_type=jnp.float32)
    for z in range(nz):
        out_ref[z] = total


def row_squares(own, oth):
    nx, half, part = own.shape
    shape = (NZ, 8, 2 * half)
    return pl.pallas_call(
        squares_kernel,
        in_specs=[VMEM] * 2,
        out_specs=VMEM,
        out_shape=jax.ShapeDtypeStruct(shape, jnp.float32),
        compiler_params=PARAMS,
        cost_estimate=cost(4 * nx * half * part, 8 * nx * half * part),
    )(own, oth)


def momentum_kernel(mine_ref, square_ref, m_ref, g_ref, own_ref, oth_ref, out_ref):
    left = scaled(mine_ref, row((1.0 - carry_keep) / square_ref[...]))
    out_ref[...] = m_ref[...] + g_ref[...].astype(jnp.float32) - product(left, own_ref, oth_ref)


def momentum_out(mine, square, momentum, gradient, own, oth):
    rows, cols = momentum.shape
    half, part = own.shape[1:]
    block = pl.BlockSpec((rows, part), lambda j: (0, j))
    right = pl.BlockSpec((1, half, part), lambda j: (j, 0, 0))
    whole = [pl.BlockSpec(array.shape, lambda j: (0, 0)) for array in (mine, square)]
    return pl.pallas_call(
        momentum_kernel,
        grid=(NX,),
        in_specs=[*whole, block, block, right, right],
        out_specs=block,
        out_shape=jax.ShapeDtypeStruct((rows, cols), jnp.float32),
        compiler_params=PARAMS,
        cost_estimate=cost(12 * rows * cols * half, 4 * (3 * rows + 2 * half) * cols),
    )(mine, square, momentum, gradient, own, oth)


def update_kernel(
    mine_ref, square_ref, sums_ref, own_ref, oth_ref, u_out, b_out, u_buf, b_buf, sems
):
    (ranks, _), (half, part) = b_buf.shape, own_ref.shape[1:]
    square = square_ref[...]
    right_scale = jnp.sqrt(sums_ref[...] / square + norm_eps)
    left = scaled(mine_ref, row(math.sqrt(ROWS * COLS / RANK) / (square * right_scale)))
    first = (lax.axis_index("y") * NX + lax.axis_index("x")) * ranks
    group = pl.multiple_of(first // 8 * 8, 8)
    lane = lax.broadcasted_iota(jnp.int32, (8, half), 1)
    rank = lax.broadcasted_iota(jnp.int32, (8, half), 0) + group
    scale = 1.0 / (jnp.sqrt(square[:1]) * right_scale[:1])
    scale = jnp.sum(jnp.where(lane == rank, scale, 0.0), axis=1, keepdims=True)

    copies = []
    for j in range(NX):
        columns = pl.ds(j * part, part)
        eight = own_ref[j, pl.ds(group, 8), :] * scale
        b_buf[:, columns] = jnp.where(first > group, eight[8 - ranks :], eight[:ranks])
    copies.append(pltpu.make_async_copy(b_buf, b_out, sems.at[NX]))
    copies[-1].start()
    for j in range(NX):
        columns = pl.ds(j * part, part)
        u_buf[:, columns] = product(left, own_ref, oth_ref, j).astype(jnp.bfloat16)
        at = (slice(None), columns)
        copies.append(pltpu.make_async_copy(u_buf.at[at], u_out.at[at], sems.at[j]))
        copies[-1].start()
    for copy in copies:
        copy.wait()


def update_out(mine, square, sums, own, oth, ranks):
    rows, (half, part) = mine.shape[0], own.shape[1:]
    cols = NX * part
    shapes = [((rows, cols), jnp.bfloat16), ((ranks, cols), jnp.float32)]
    return pl.pallas_call(
        update_kernel,
        in_specs=[VMEM] * 5,
        out_specs=[HBM] * 2,
        out_shape=[jax.ShapeDtypeStruct(*shape) for shape in shapes],
        scratch_shapes=[pltpu.VMEM(*shape) for shape in shapes]
        + [pltpu.SemaphoreType.DMA((NX + 1,))],
        compiler_params=PARAMS,
        cost_estimate=cost(12 * rows * cols * half, 4 * (rows + 2 * half) * cols),
    )(mine, square, sums, own, oth)


def exchange(blocks, axes):
    return lax.all_to_all(blocks, axes, 0, 0, tiled=True)


def spread(block, axes, n):
    return exchange(jnp.broadcast_to(block[None], (n, *block.shape)), axes)


def shards(momentum, gradient, basis_panel):
    rows, cols = momentum.shape
    rank_rows = basis_panel.shape[0]
    part = cols // NX
    half = NY * NX * rank_rows
    own_ranks = NX * rank_rows
    padded = -(-rows // (8 * NZ)) * 8 * NZ

    blocks = deal(momentum, gradient)
    pieces = basis_pieces(basis_panel, blocks[0])
    blocks = [blocks[0]] + [
        lax.ppermute(blocks[j], "x", [(i, (i + j) % NX) for i in range(NX)]) for j in range(1, NX)
    ]
    basis_own = exchange(pieces, ("y", "x"))
    basis_own, *tall = lax.optimization_barrier((basis_own, *tall_parts(blocks)))
    basis_own = basis_own.reshape(half, part)
    basis_oth = lax.ppermute(basis_own, "core", SWAP)

    panel = [panel_part(tall, basis, padded) for basis in (basis_own, basis_oth)]
    panel = jnp.concatenate(panel, axis=2)
    panel = exchange(panel.reshape(NX * NZ, padded // NZ, 2 * half), ("x", "z"))
    panel = spread(jnp.sum(panel, axis=0), ("x", "z"), NX * NZ)
    panel = panel.reshape(NX, padded, 2 * half)

    right_oth = lax.ppermute(right_part(1, tall, panel)[0], "core", SWAP)
    right_sum, mine = right_part(0, tall, panel)
    right_sum = right_sum + right_oth
    square = right_sum[half, : 2 * half].reshape(2, half)
    right_sum = exchange(right_sum[:half].reshape(NY, own_ranks, part), "y")
    right_sum = jnp.sum(right_sum, axis=0)
    beside = jnp.zeros((own_ranks, 128), jnp.float32).at[:2, :half].set(square)
    got = spread(jnp.concatenate([right_sum, beside], axis=1), "y", NY)
    square = jnp.sum(got[:, :2, part : part + half], axis=0) + norm_eps

    own, square = lax.optimization_barrier((got[:, :, :part].reshape(half, part), square))
    own = spread(own, "x", NX)
    own, oth = lax.optimization_barrier((own, lax.ppermute(own, "core", SWAP)))
    sums = jnp.sum(exchange(row_squares(own, oth), "z"), axis=0)[0].reshape(2, half)

    momentum_new = momentum_out(mine, square, momentum, gradient, own, oth)
    update, basis_new = update_out(mine, square, sums, own, oth, rank_rows)
    return momentum_new, basis_new, update


def solution(mesh):
    fine = Mesh(mesh.devices.reshape(NY, NX, NC, NZ), ("y", "x", "core", "z"))
    spec = P(("y", "x", "core"), "z")
    return jax.shard_map(
        shards,
        mesh=fine,
        in_specs=(spec, spec, spec),
        out_specs=(spec, spec, spec),
        check_vma=False,
    )
```

```python
import functools
import math

import jax
import jax.numpy as jnp
import numpy as np
from jax import lax
from jax.experimental import pallas as pl
from jax.experimental.pallas import tpu as pltpu
from jax.sharding import Mesh, PartitionSpec as P

ROWS = 7168
COLS = 28672
RANK = 256

NY, NX, NC, NZ = 8, 4, 2, 8

norm_eps = 1e-06
carry_keep = 0.9
SWAP = [(0, 1), (1, 0)]
PARAMS = pltpu.CompilerParams(vmem_limit_bytes=12 * 1024 * 1024)
VMEM = pl.BlockSpec(memory_space=pltpu.VMEM)
ANY = pl.BlockSpec(memory_space=pl.ANY)
HBM = pl.BlockSpec(memory_space=pltpu.HBM)


def split(value):
    high = value.astype(jnp.bfloat16)
    return high, (value - high.astype(jnp.float32)).astype(jnp.bfloat16)


def dot3(a, b, dims):
    dot = functools.partial(
        lax.dot_general, dimension_numbers=(dims, ((), ())), preferred_element_type=jnp.float32
    )
    return dot(a[1], b[0]) + dot(a[0], b[1]) + dot(a[0], b[0])


def cost(flops, nbytes):
    return pl.CostEstimate(flops=flops, bytes_accessed=nbytes, transcendentals=0)


def deal_kernel(m_ref, g_ref, *refs):
    blocks, (m_buf, g_buf, sems) = refs[:NX], refs[NX:]
    part = blocks[0].shape[1]
    loads = []
    for j in range(NX):
        at = lax.rem(lax.axis_index("x") + j, NX)
        columns = (slice(None), pl.ds(pl.multiple_of(at * part, 128), part))
        loads.append(
            (
                pltpu.make_async_copy(m_ref.at[columns], m_buf.at[j], sems.at[j, 0]),
                pltpu.make_async_copy(g_ref.at[columns], g_buf.at[j], sems.at[j, 1]),
            )
        )
    for j in (*range(1, NX), 0):
        for load in loads[j]:
            load.start()
    for j in (*range(1, NX), 0):
        for load in loads[j]:
            load.wait()
        blocks[j][...] = m_buf[j] + g_buf[j].astype(jnp.float32)


def deal(momentum, gradient):
    rows, cols = momentum.shape
    part = cols // NX
    return pl.pallas_call(
        deal_kernel,
        in_specs=[HBM] * 2,
        out_specs=[VMEM] * NX,
        out_shape=[jax.ShapeDtypeStruct((rows, part), jnp.float32)] * NX,
        scratch_shapes=[
            pltpu.VMEM((NX, rows, part), jnp.float32),
            pltpu.VMEM((NX, rows, part), jnp.bfloat16),
            pltpu.SemaphoreType.DMA((NX, 2)),
        ],
        compiler_params=PARAMS,
        cost_estimate=cost(rows * cols, 10 * rows * cols),
    )(momentum, gradient)


def pieces_kernel(basis_ref, after_ref, pieces_ref):
    part = pieces_ref.shape[2]
    for to in range(NX):
        piece = basis_ref[:, to * part : (to + 1) * part]
        for y in range(NY):
            pieces_ref[y * NX + to] = piece


def basis_pieces(basis, after):
    ranks, cols = basis.shape
    pieces = (NY * NX, ranks, cols // NX)
    return pl.pallas_call(
        pieces_kernel,
        in_specs=[VMEM, ANY],
        out_specs=VMEM,
        out_shape=jax.ShapeDtypeStruct(pieces, jnp.float32),
        compiler_params=PARAMS,
        cost_estimate=cost(10**10, 10**8),
    )(basis, after)


def tall_kernel(*refs):
    blocks, (high_ref, low_ref) = refs[:NX], refs[NX:]
    rows = blocks[0].shape[0]
    for j, ref in enumerate(blocks):
        at = slice(j * rows, (j + 1) * rows)
        high_ref[at], low_ref[at] = split(ref[...])


def tall_parts(blocks):
    rows, part = blocks[0].shape
    shape = jax.ShapeDtypeStruct((NX * rows, part), jnp.bfloat16)
    return pl.pallas_call(
        tall_kernel,
        in_specs=[VMEM] * NX,
        out_specs=[VMEM] * 2,
        out_shape=[shape] * 2,
        compiler_params=PARAMS,
        cost_estimate=cost(10**10, 2 * 10**8),
    )(*blocks)


def panel_kernel(high_ref, low_ref, basis_ref, out_ref):
    rows = high_ref.shape[0] // NX
    panel = dot3((high_ref[...], low_ref[...]), split(basis_ref[...]), ((1,), (1,)))
    for j in range(NX):
        at = lax.rem(lax.axis_index("x") + (NX - j), NX)
        out_ref[at, :rows] = panel[j * rows : (j + 1) * rows]
        if out_ref.shape[1] > rows:
            spare = (out_ref.shape[1] - rows, out_ref.shape[2])
            out_ref[at, rows:] = jnp.zeros(spare, jnp.float32)


def panel_part(tall, basis, padded):
    rows, part = tall[0].shape
    half = basis.shape[0]
    return pl.pallas_call(
        panel_kernel,
        in_specs=[VMEM] * 3,
        out_specs=VMEM,
        out_shape=jax.ShapeDtypeStruct((NX, padded, half), jnp.float32),
        compiler_params=PARAMS,
        cost_estimate=cost(6 * rows * part * half, 4 * (rows + half) * part),
    )(*tall, basis)


def right_kernel(side, high_ref, low_ref, panel_ref, out_ref, mine_ref=None):
    rows, half = high_ref.shape[0] // NX, panel_ref.shape[2] // 2
    tall = (high_ref[...], low_ref[...])
    panel = [panel_ref[lax.rem(lax.axis_index("x") + (NX - j), NX), :rows] for j in range(NX)]
    if side == 0:
        mine_ref[...] = panel[0]
    panel = jnp.concatenate(panel, axis=0)
    out_ref[half:] = jnp.zeros((8, out_ref.shape[1]), jnp.float32)
    squares = jnp.sum(panel * panel, axis=0, keepdims=True)
    out_ref[half : half + 1, :half] = squares[:, side * half : (side + 1) * half]
    out_ref[half : half + 1, half : 2 * half] = squares[:, (1 - side) * half : (2 - side) * half]
    panel = panel[:, side * half : (side + 1) * half]
    out_ref[:half] = dot3(split(panel), tall, ((0,), (0,)))


def right_part(side, tall, panel):
    rows, part = tall[0].shape
    half = panel.shape[2] // 2
    shapes = [(half + 8, part), (rows // NX, 2 * half)][: 2 - side]
    return pl.pallas_call(
        functools.partial(right_kernel, side),
        in_specs=[VMEM] * 3,
        out_specs=[VMEM] * len(shapes),
        out_shape=[jax.ShapeDtypeStruct(shape, jnp.float32) for shape in shapes],
        compiler_params=PARAMS,
        cost_estimate=cost(6 * rows * part * half, 4 * rows * part),
    )(*tall, panel)


def row(pair):
    return jnp.concatenate([pair[:1], pair[1:2]], axis=1)


def squares_kernel(own_ref, out_ref):
    nz, lines, _ = out_ref.shape
    part = own_ref.shape[2]
    ones = jnp.ones((lines, part), jnp.bfloat16)
    total = 0.0
    for j in range(NX):
        for piece in split(own_ref[j] * own_ref[j]):
            dims = (((1,), (1,)), ((), ()))
            total += lax.dot_general(ones, piece, dims, preferred_element_type=jnp.float32)
    for z in range(nz):
        out_ref[z] = total


def row_squares(own):
    nx, half, part = own.shape
    return pl.pallas_call(
        squares_kernel,
        in_specs=[VMEM],
        out_specs=VMEM,
        out_shape=jax.ShapeDtypeStruct((NC * NZ, 8, half), jnp.float32),
        compiler_params=PARAMS,
        cost_estimate=cost(4 * nx * half * part, 4 * nx * half * part),
    )(own)


def last_kernel(
    mine_ref, square_ref, sums_ref, m_ref, g_ref, own_ref, oth_ref,
    m_out, u_out, b_out, m_buf, u_buf, b_buf, sems,
):
    rows, (ranks, _), (half, part) = mine_ref.shape[0], b_buf.shape, own_ref.shape[1:]
    core = lax.axis_index("core")
    square = square_ref[...]
    sums = []
    for side in (core, 1 - core):
        total = sums_ref[side * NZ]
        for z in range(1, NZ):
            total = total + sums_ref[side * NZ + z]
        sums.append(total[:1])
    right_scale = jnp.sqrt(jnp.concatenate(sums, axis=0) / square + norm_eps)
    panel = mine_ref[...]
    m_left = split(panel * row((1.0 - carry_keep) / square))
    u_left = split(panel * row(math.sqrt(ROWS * COLS / RANK) / (square * right_scale)))
    left = jnp.concatenate([*m_left, *u_left], axis=0)
    left_high = jnp.concatenate([m_left[0], u_left[0]], axis=0)
    first = (lax.axis_index("y") * NX + lax.axis_index("x")) * ranks
    group = pl.multiple_of(first // 8 * 8, 8)
    lane = lax.broadcasted_iota(jnp.int32, (8, half), 1)
    rank = lax.broadcasted_iota(jnp.int32, (8, half), 0) + group
    scale = 1.0 / (jnp.sqrt(square[:1]) * right_scale[:1])
    scale = jnp.sum(jnp.where(lane == rank, scale, 0.0), axis=1, keepdims=True)

    dot = functools.partial(jnp.dot, preferred_element_type=jnp.float32)
    copies = []
    for j in range(NX):
        own_at = jnp.where(core == 0, j, NX - 1 - j)
        own, columns = own_ref[own_at], pl.ds(j * part, part)
        high, low = split(jnp.concatenate([own, oth_ref[NX - 1 - own_at]], axis=0))
        sums, rest = dot(left, high), dot(left_high, low)
        feedback = sums[:rows] + sums[rows : 2 * rows] + rest[:rows]
        update = sums[2 * rows : 3 * rows] + sums[3 * rows :] + rest[rows:]
        combined = m_ref[:, columns] + g_ref[:, columns].astype(jnp.float32)
        m_buf[:, columns] = combined - feedback
        u_buf[:, columns] = update.astype(jnp.bfloat16)
        eight = own_ref[own_at, pl.ds(group, 8), :] * scale
        b_buf[:, columns] = jnp.where(first > group, eight[8 - ranks :], eight[:ranks])
        at = (slice(None), columns)
        for i, (buf, out) in enumerate(((m_buf, m_out), (u_buf, u_out))):
            copies.append(pltpu.make_async_copy(buf.at[at], out.at[at], sems.at[j, i]))
            copies[-1].start()
    copies.append(pltpu.make_async_copy(b_buf, b_out, sems.at[NX, 0]))
    copies[-1].start()
    for copy in copies:
        copy.wait()


def last_out(mine, square, sums, momentum, gradient, own, oth, ranks):
    rows, cols = momentum.shape
    half = own.shape[1]
    shapes = [
        ((rows, cols), jnp.float32),
        ((rows, cols), jnp.bfloat16),
        ((ranks, cols), jnp.float32),
    ]
    return pl.pallas_call(
        last_kernel,
        in_specs=[VMEM] * 7,
        out_specs=[HBM] * 3,
        out_shape=[jax.ShapeDtypeStruct(*shape) for shape in shapes],
        scratch_shapes=[pltpu.VMEM(*shape) for shape in shapes]
        + [pltpu.SemaphoreType.DMA((NX + 1, 2))],
        compiler_params=PARAMS,
        cost_estimate=cost(24 * rows * cols * half, 4 * (4 * rows + 2 * half) * cols),
    )(mine, square, sums, momentum, gradient, own, oth)


def exchange(blocks, axes):
    return lax.all_to_all(blocks, axes, 0, 0, tiled=True)


def opposed(blocks, axes):
    sizes = {"y": NY, "x": NX, "core": NC, "z": NZ}
    at = np.arange(math.prod(sizes[axis] for axis in axes)).reshape([sizes[axis] for axis in axes])
    at = np.moveaxis(at, axes.index("core"), 0).reshape(NC, -1)
    groups = [at[0].tolist(), at[1, ::-1].tolist()]
    return lax.all_to_all(blocks, axes, 0, 0, axis_index_groups=groups, tiled=True)


def spread(block, axes, n):
    return opposed(jnp.broadcast_to(block[None], (n, *block.shape)), axes)


def shards(momentum, gradient, basis_panel):
    rows, cols = momentum.shape
    rank_rows = basis_panel.shape[0]
    part = cols // NX
    half = NY * NX * rank_rows
    own_ranks = NX * rank_rows
    padded = -(-rows // (8 * NZ)) * 8 * NZ

    blocks = deal(momentum, gradient)
    pieces = basis_pieces(basis_panel, blocks[0])
    blocks = [blocks[0]] + [
        lax.ppermute(blocks[j], "x", [(i, (i + j) % NX) for i in range(NX)]) for j in range(1, NX)
    ]
    basis_own = exchange(pieces, ("y", "x"))
    basis_own, *tall = lax.optimization_barrier((basis_own, *tall_parts(blocks)))
    basis_own = basis_own.reshape(half, part)
    basis_oth = lax.ppermute(basis_own, "core", SWAP)

    panel = [panel_part(tall, basis, padded) for basis in (basis_own, basis_oth)]
    panel = jnp.concatenate(panel, axis=2)
    panel = opposed(panel.reshape(NX * NZ, padded // NZ, 2 * half), ("x", "core", "z"))
    panel = spread(jnp.sum(panel, axis=0), ("x", "core", "z"), NX * NZ)
    panel = panel.reshape(NX, padded, 2 * half)

    right_oth = lax.ppermute(right_part(1, tall, panel)[0], "core", SWAP)
    right_sum, mine = right_part(0, tall, panel)
    right_sum = right_sum + right_oth
    square = right_sum[half, : 2 * half].reshape(2, half)
    right_sum, square = lax.optimization_barrier((right_sum[:half], square))
    right_sum = opposed(right_sum.reshape(NY, own_ranks, part), ("y", "core"))
    right_sum = jnp.sum(right_sum, axis=0)
    beside = jnp.zeros((own_ranks, 128), jnp.float32).at[:2, :half].set(square)
    got = spread(jnp.concatenate([right_sum, beside], axis=1), ("y", "core"), NY)
    square = jnp.sum(got[:, :2, part : part + half], axis=0) + norm_eps

    own, square = lax.optimization_barrier((got[:, :, :part].reshape(half, part), square))
    own = spread(own, ("x", "core"), NX)
    oth = lax.ppermute(own, "core", SWAP)
    sums = exchange(row_squares(own), ("core", "z"))
    momentum_new, update, basis_new = last_out(
        mine, square, sums, momentum, gradient, own, oth, rank_rows
    )
    return momentum_new, basis_new, update


def solution(mesh):
    fine = Mesh(mesh.devices.reshape(NY, NX, NC, NZ), ("y", "x", "core", "z"))
    spec = P(("y", "x", "core"), "z")
    return jax.shard_map(
        shards,
        mesh=fine,
        in_specs=(spec, spec, spec),
        out_specs=(spec, spec, spec),
        check_vma=False,
    )
```

```python
import functools
import math

import jax
import jax.numpy as jnp
import numpy as np
from jax import lax
from jax.experimental import pallas as pl
from jax.experimental.pallas import tpu as pltpu
from jax.sharding import Mesh, PartitionSpec as P

ROWS = 7168
COLS = 28672
RANK = 256

NY, NX, NC, NZ = 8, 4, 2, 8

norm_eps = 1e-06
carry_keep = 0.9
SWAP = [(0, 1), (1, 0)]
PARAMS = pltpu.CompilerParams(vmem_limit_bytes=12 * 1024 * 1024)
VMEM = pl.BlockSpec(memory_space=pltpu.VMEM)
ANY = pl.BlockSpec(memory_space=pl.ANY)
HBM = pl.BlockSpec(memory_space=pltpu.HBM)


def split(value):
    high = value.astype(jnp.bfloat16)
    return high, (value - high.astype(jnp.float32)).astype(jnp.bfloat16)


def dot3(a, b, dims):
    dot = functools.partial(
        lax.dot_general, dimension_numbers=(dims, ((), ())), preferred_element_type=jnp.float32
    )
    return dot(a[1], b[0]) + dot(a[0], b[1]) + dot(a[0], b[0])


def cost(flops, nbytes):
    return pl.CostEstimate(flops=flops, bytes_accessed=nbytes, transcendentals=0)


def deal_kernel(c_ref, *blocks):
    part = blocks[0].shape[1]
    for j, ref in enumerate(blocks):
        at = lax.rem(lax.axis_index("x") + j, NX)
        ref[...] = c_ref[:, pl.ds(pl.multiple_of(at * part, 128), part)]


def deal(combined):
    rows, cols = combined.shape
    part = cols // NX
    return pl.pallas_call(
        deal_kernel,
        in_specs=[VMEM],
        out_specs=[VMEM] * NX,
        out_shape=[jax.ShapeDtypeStruct((rows, part), jnp.float32)] * NX,
        compiler_params=PARAMS,
        cost_estimate=cost(rows * cols, 8 * rows * cols),
    )(combined)


def pieces_kernel(basis_ref, after_ref, pieces_ref):
    part = pieces_ref.shape[2]
    for to in range(NX):
        piece = basis_ref[:, to * part : (to + 1) * part]
        for y in range(NY):
            pieces_ref[y * NX + to] = piece


def basis_pieces(basis, after):
    ranks, cols = basis.shape
    pieces = (NY * NX, ranks, cols // NX)
    return pl.pallas_call(
        pieces_kernel,
        in_specs=[VMEM, ANY],
        out_specs=VMEM,
        out_shape=jax.ShapeDtypeStruct(pieces, jnp.float32),
        compiler_params=PARAMS,
        cost_estimate=cost(10**10, 10**8),
    )(basis, after)


def tall_kernel(*refs):
    blocks, (high_ref, low_ref) = refs[:NX], refs[NX:]
    rows = blocks[0].shape[0]
    for j, ref in enumerate(blocks):
        at = slice(j * rows, (j + 1) * rows)
        high_ref[at], low_ref[at] = split(ref[...])


def tall_parts(blocks):
    rows, part = blocks[0].shape
    shape = jax.ShapeDtypeStruct((NX * rows, part), jnp.bfloat16)
    return pl.pallas_call(
        tall_kernel,
        in_specs=[VMEM] * NX,
        out_specs=[VMEM] * 2,
        out_shape=[shape] * 2,
        compiler_params=PARAMS,
        cost_estimate=cost(10**10, 2 * 10**8),
    )(*blocks)


def panel_kernel(high_ref, low_ref, basis_ref, out_ref, buf):
    rows = high_ref.shape[0] // NX
    n, ranks, _ = basis_ref.shape
    for i in range(n):
        buf[i * ranks : (i + 1) * ranks] = basis_ref[i]
    panel = dot3((high_ref[...], low_ref[...]), split(buf[...]), ((1,), (1,)))
    for j in range(NX):
        at = lax.rem(lax.axis_index("x") + (NX - j), NX)
        out_ref[at, :rows] = panel[j * rows : (j + 1) * rows]
        if out_ref.shape[1] > rows:
            spare = (out_ref.shape[1] - rows, out_ref.shape[2])
            out_ref[at, rows:] = jnp.zeros(spare, jnp.float32)


def panel_part(tall, basis, padded):
    rows, part = tall[0].shape
    half = basis.shape[0] * basis.shape[1]
    return pl.pallas_call(
        panel_kernel,
        in_specs=[VMEM] * 3,
        out_specs=VMEM,
        out_shape=jax.ShapeDtypeStruct((NX, padded, half), jnp.float32),
        scratch_shapes=[pltpu.VMEM((half, part), jnp.float32)],
        compiler_params=PARAMS,
        cost_estimate=cost(6 * rows * part * half, 4 * (rows + half) * part),
    )(*tall, basis)


def right_kernel(side, high_ref, low_ref, panel_ref, out_ref, mine_ref=None):
    rows, half = high_ref.shape[0] // NX, panel_ref.shape[2] // 2
    tall = (high_ref[...], low_ref[...])
    panel = [panel_ref[lax.rem(lax.axis_index("x") + (NX - j), NX), :rows] for j in range(NX)]
    if side == 0:
        mine_ref[...] = panel[0]
    panel = jnp.concatenate(panel, axis=0)
    out_ref[half:] = jnp.zeros((8, out_ref.shape[1]), jnp.float32)
    squares = jnp.sum(panel * panel, axis=0, keepdims=True)
    out_ref[half : half + 1, :half] = squares[:, side * half : (side + 1) * half]
    out_ref[half : half + 1, half : 2 * half] = squares[:, (1 - side) * half : (2 - side) * half]
    panel = panel[:, side * half : (side + 1) * half]
    out_ref[:half] = dot3(split(panel), tall, ((0,), (0,)))


def right_part(side, tall, panel):
    rows, part = tall[0].shape
    half = panel.shape[2] // 2
    shapes = [(half + 8, part), (rows // NX, 2 * half)][: 2 - side]
    return pl.pallas_call(
        functools.partial(right_kernel, side),
        in_specs=[VMEM] * 3,
        out_specs=[VMEM] * len(shapes),
        out_shape=[jax.ShapeDtypeStruct(shape, jnp.float32) for shape in shapes],
        compiler_params=PARAMS,
        cost_estimate=cost(6 * rows * part * half, 4 * rows * part),
    )(*tall, panel)


def row(pair):
    return jnp.concatenate([pair[:1], pair[1:2]], axis=1)


def squares_kernel(own_ref, out_ref):
    nz, lines, _ = out_ref.shape
    part = own_ref.shape[2]
    ones = jnp.ones((lines, part), jnp.bfloat16)
    total = 0.0
    for j in range(NX):
        for piece in split(own_ref[j] * own_ref[j]):
            dims = (((1,), (1,)), ((), ()))
            total += lax.dot_general(ones, piece, dims, preferred_element_type=jnp.float32)
    for z in range(nz):
        out_ref[z] = total


def row_squares(own):
    nx, half, part = own.shape
    return pl.pallas_call(
        squares_kernel,
        in_specs=[VMEM],
        out_specs=VMEM,
        out_shape=jax.ShapeDtypeStruct((NC * NZ, 8, half), jnp.float32),
        compiler_params=PARAMS,
        cost_estimate=cost(4 * nx * half * part, 4 * nx * half * part),
    )(own)


def last_kernel(
    mine_ref, square_ref, sums_ref, m_ref, g_ref, own_ref, oth_ref,
    m_out, u_out, b_out, m_buf, u_buf, b_buf, sems,
):
    rows, (ranks, _), (half, part) = mine_ref.shape[0], b_buf.shape, own_ref.shape[1:]
    core = lax.axis_index("core")
    square = square_ref[...]
    sums = []
    for side in (core, 1 - core):
        total = sums_ref[side * NZ]
        for z in range(1, NZ):
            total = total + sums_ref[side * NZ + z]
        sums.append(total[:1])
    right_scale = jnp.sqrt(jnp.concatenate(sums, axis=0) / square + norm_eps)
    panel = mine_ref[...]
    m_left = split(panel * row((1.0 - carry_keep) / square))
    u_left = split(panel * row(math.sqrt(ROWS * COLS / RANK) / (square * right_scale)))
    left = jnp.concatenate([*m_left, *u_left], axis=0)
    left_high = jnp.concatenate([m_left[0], u_left[0]], axis=0)
    first = (lax.axis_index("y") * NX + lax.axis_index("x")) * ranks
    group = pl.multiple_of(first // 8 * 8, 8)
    lane = lax.broadcasted_iota(jnp.int32, (8, half), 1)
    rank = lax.broadcasted_iota(jnp.int32, (8, half), 0) + group
    scale = 1.0 / (jnp.sqrt(square[:1]) * right_scale[:1])
    scale = jnp.sum(jnp.where(lane == rank, scale, 0.0), axis=1, keepdims=True)

    dot = functools.partial(jnp.dot, preferred_element_type=jnp.float32)
    copies = []
    for j in range(NX):
        own_at = jnp.where(core == 0, j, NX - 1 - j)
        own, columns = own_ref[own_at], pl.ds(j * part, part)
        high, low = split(jnp.concatenate([own, oth_ref[NX - 1 - own_at]], axis=0))
        sums, rest = dot(left, high), dot(left_high, low)
        feedback = sums[:rows] + sums[rows : 2 * rows] + rest[:rows]
        update = sums[2 * rows : 3 * rows] + sums[3 * rows :] + rest[rows:]
        combined = m_ref[:, columns] + g_ref[:, columns].astype(jnp.float32)
        m_buf[:, columns] = combined - feedback
        u_buf[:, columns] = update.astype(jnp.bfloat16)
        eight = own_ref[own_at, pl.ds(group, 8), :] * scale
        b_buf[:, columns] = jnp.where(first > group, eight[8 - ranks :], eight[:ranks])
        at = (slice(None), columns)
        for i, (buf, out) in enumerate(((m_buf, m_out), (u_buf, u_out))):
            copies.append(pltpu.make_async_copy(buf.at[at], out.at[at], sems.at[j, i]))
            copies[-1].start()
    copies.append(pltpu.make_async_copy(b_buf, b_out, sems.at[NX, 0]))
    copies[-1].start()
    for copy in copies:
        copy.wait()


def last_out(mine, square, sums, momentum, gradient, own, oth, ranks):
    rows, cols = momentum.shape
    half = own.shape[1]
    shapes = [
        ((rows, cols), jnp.float32),
        ((rows, cols), jnp.bfloat16),
        ((ranks, cols), jnp.float32),
    ]
    return pl.pallas_call(
        last_kernel,
        in_specs=[VMEM] * 7,
        out_specs=[HBM] * 3,
        out_shape=[jax.ShapeDtypeStruct(*shape) for shape in shapes],
        scratch_shapes=[pltpu.VMEM(*shape) for shape in shapes]
        + [pltpu.SemaphoreType.DMA((NX + 1, 2))],
        compiler_params=PARAMS,
        cost_estimate=cost(24 * rows * cols * half, 4 * (4 * rows + 2 * half) * cols),
    )(mine, square, sums, momentum, gradient, own, oth)


def exchange(blocks, axes):
    return lax.all_to_all(blocks, axes, 0, 0, tiled=True)


def opposed(blocks, axes):
    sizes = {"y": NY, "x": NX, "core": NC, "z": NZ}
    at = np.arange(math.prod(sizes[axis] for axis in axes)).reshape([sizes[axis] for axis in axes])
    at = np.moveaxis(at, axes.index("core"), 0).reshape(NC, -1)
    groups = [at[0].tolist(), at[1, ::-1].tolist()]
    return lax.all_to_all(blocks, axes, 0, 0, axis_index_groups=groups, tiled=True)


def spread(block, axes, n):
    return opposed(jnp.broadcast_to(block[None], (n, *block.shape)), axes)


def shards(momentum, gradient, basis_panel):
    rows, cols = momentum.shape
    rank_rows = basis_panel.shape[0]
    part = cols // NX
    half = NY * NX * rank_rows
    own_ranks = NX * rank_rows
    padded = -(-rows // (8 * NZ)) * 8 * NZ

    blocks = deal(momentum + gradient.astype(jnp.float32))
    pieces = basis_pieces(basis_panel, blocks[0])
    blocks = [blocks[0]] + [
        lax.ppermute(blocks[j], "x", [(i, (i + j) % NX) for i in range(NX)]) for j in range(1, NX)
    ]
    basis_own = exchange(pieces, ("y", "x"))
    basis_own, *tall = lax.optimization_barrier((basis_own, *tall_parts(blocks)))
    basis_oth = lax.ppermute(basis_own, "core", SWAP)

    panel = [panel_part(tall, basis, padded) for basis in (basis_own, basis_oth)]
    panel = jnp.concatenate(panel, axis=2)
    panel = opposed(panel.reshape(NX * NZ, padded // NZ, 2 * half), ("x", "core", "z"))
    panel = spread(jnp.sum(panel, axis=0), ("x", "core", "z"), NX * NZ)
    panel = panel.reshape(NX, padded, 2 * half)

    right_oth = lax.ppermute(right_part(1, tall, panel)[0], "core", SWAP)
    right_sum, mine = right_part(0, tall, panel)
    right_sum = right_sum + right_oth
    square = right_sum[half, : 2 * half].reshape(2, half)
    right_sum, square = lax.optimization_barrier((right_sum[:half], square))
    right_sum = opposed(right_sum.reshape(NY, own_ranks, part), ("y", "core"))
    right_sum = jnp.sum(right_sum, axis=0)
    beside = jnp.zeros((own_ranks, 128), jnp.float32).at[:2, :half].set(square)
    got = spread(jnp.concatenate([right_sum, beside], axis=1), ("y", "core"), NY)
    square = jnp.sum(got[:, :2, part : part + half], axis=0) + norm_eps

    own, square = lax.optimization_barrier((got[:, :, :part].reshape(half, part), square))
    own = spread(own, ("x", "core"), NX)
    oth = lax.ppermute(own, "core", SWAP)
    sums = exchange(row_squares(own), ("core", "z"))
    momentum_new, update, basis_new = last_out(
        mine, square, sums, momentum, gradient, own, oth, rank_rows
    )
    return momentum_new, basis_new, update


def solution(mesh):
    fine = Mesh(mesh.devices.reshape(NY, NX, NC, NZ), ("y", "x", "core", "z"))
    spec = P(("y", "x", "core"), "z")
    return jax.shard_map(
        shards,
        mesh=fine,
        in_specs=(spec, spec, spec),
        out_specs=(spec, spec, spec),
        check_vma=False,
    )
```

```python
import functools
import math

import jax
import jax.numpy as jnp
import numpy as np
from jax import lax
from jax.experimental import pallas as pl
from jax.experimental.pallas import tpu as pltpu
from jax.sharding import Mesh, PartitionSpec as P

ROWS = 7168
COLS = 28672
RANK = 256

NY, NX, NC, NZ = 8, 4, 2, 8

norm_eps = 1e-06
carry_keep = 0.9
SWAP = [(0, 1), (1, 0)]
PARAMS = pltpu.CompilerParams(vmem_limit_bytes=12 * 1024 * 1024)
VMEM = pl.BlockSpec(memory_space=pltpu.VMEM)
ANY = pl.BlockSpec(memory_space=pl.ANY)
HBM = pl.BlockSpec(memory_space=pltpu.HBM)


def split(value):
    high = value.astype(jnp.bfloat16)
    return high, (value - high.astype(jnp.float32)).astype(jnp.bfloat16)


def dot3(a, b, dims):
    dot = functools.partial(
        lax.dot_general, dimension_numbers=(dims, ((), ())), preferred_element_type=jnp.float32
    )
    return dot(a[1], b[0]) + dot(a[0], b[1]) + dot(a[0], b[0])


def cost(flops, nbytes):
    return pl.CostEstimate(flops=flops, bytes_accessed=nbytes, transcendentals=0)


def x_away(j):
    steps = jnp.where(lax.axis_index("core") == 0, j, NX - j)
    return lax.rem(lax.axis_index("x") + steps, NX)


def deal_kernel(c_ref, *blocks):
    part = blocks[0].shape[1]
    for j, ref in enumerate(blocks):
        at = x_away(j)
        ref[...] = c_ref[:, pl.ds(pl.multiple_of(at * part, 128), part)]


def deal(combined):
    rows, cols = combined.shape
    part = cols // NX
    return pl.pallas_call(
        deal_kernel,
        in_specs=[VMEM],
        out_specs=[VMEM] * NX,
        out_shape=[jax.ShapeDtypeStruct((rows, part), jnp.float32)] * NX,
        compiler_params=PARAMS,
        cost_estimate=cost(rows * cols, 8 * rows * cols),
    )(combined)


def pieces_kernel(basis_ref, after_ref, pieces_ref):
    part = pieces_ref.shape[2]
    for to in range(NX):
        at = jnp.where(lax.axis_index("core") == 0, to, NX - 1 - to)
        piece = basis_ref[:, pl.ds(pl.multiple_of(at * part, 128), part)]
        for y in range(NY):
            pieces_ref[y * NX + to] = piece


def basis_pieces(basis, after):
    ranks, cols = basis.shape
    pieces = (NY * NX, ranks, cols // NX)
    return pl.pallas_call(
        pieces_kernel,
        in_specs=[VMEM, ANY],
        out_specs=VMEM,
        out_shape=jax.ShapeDtypeStruct(pieces, jnp.float32),
        compiler_params=PARAMS,
        cost_estimate=cost(10**10, 10**8),
    )(basis, after)


def tall_kernel(*refs):
    blocks, (high_ref, low_ref) = refs[:NX], refs[NX:]
    rows = blocks[0].shape[0]
    for j, ref in enumerate(blocks):
        at = slice(j * rows, (j + 1) * rows)
        high_ref[at], low_ref[at] = split(ref[...])


def tall_parts(blocks):
    rows, part = blocks[0].shape
    shape = jax.ShapeDtypeStruct((NX * rows, part), jnp.bfloat16)
    return pl.pallas_call(
        tall_kernel,
        in_specs=[VMEM] * NX,
        out_specs=[VMEM] * 2,
        out_shape=[shape] * 2,
        compiler_params=PARAMS,
        cost_estimate=cost(10**10, 2 * 10**8),
    )(*blocks)


def panel_kernel(high_ref, low_ref, basis_ref, out_ref, buf):
    rows = high_ref.shape[0] // NX
    n, ranks, _ = basis_ref.shape
    for i in range(n):
        buf[i * ranks : (i + 1) * ranks] = basis_ref[i]
    panel = dot3((high_ref[...], low_ref[...]), split(buf[...]), ((1,), (1,)))
    for j in range(NX):
        at = x_away(NX - j)
        out_ref[at, :rows] = panel[j * rows : (j + 1) * rows]
        if out_ref.shape[1] > rows:
            spare = (out_ref.shape[1] - rows, out_ref.shape[2])
            out_ref[at, rows:] = jnp.zeros(spare, jnp.float32)


def panel_part(tall, basis, padded):
    rows, part = tall[0].shape
    half = basis.shape[0] * basis.shape[1]
    return pl.pallas_call(
        panel_kernel,
        in_specs=[VMEM] * 3,
        out_specs=VMEM,
        out_shape=jax.ShapeDtypeStruct((NX, padded, half), jnp.float32),
        scratch_shapes=[pltpu.VMEM((half, part), jnp.float32)],
        compiler_params=PARAMS,
        cost_estimate=cost(6 * rows * part * half, 4 * (rows + half) * part),
    )(*tall, basis)


def right_kernel(side, high_ref, low_ref, panel_ref, out_ref, mine_ref=None):
    rows, half = high_ref.shape[0] // NX, panel_ref.shape[2] // 2
    tall = (high_ref[...], low_ref[...])
    panel = [panel_ref[x_away(NX - j), :rows] for j in range(NX)]
    if side == 0:
        mine_ref[...] = panel[0]
    panel = jnp.concatenate(panel, axis=0)
    out_ref[half:] = jnp.zeros((8, out_ref.shape[1]), jnp.float32)
    squares = jnp.sum(panel * panel, axis=0, keepdims=True)
    out_ref[half : half + 1, :half] = squares[:, side * half : (side + 1) * half]
    out_ref[half : half + 1, half : 2 * half] = squares[:, (1 - side) * half : (2 - side) * half]
    panel = panel[:, side * half : (side + 1) * half]
    out_ref[:half] = dot3(split(panel), tall, ((0,), (0,)))


def right_part(side, tall, panel):
    rows, part = tall[0].shape
    half = panel.shape[2] // 2
    shapes = [(half + 8, part), (rows // NX, 2 * half)][: 2 - side]
    return pl.pallas_call(
        functools.partial(right_kernel, side),
        in_specs=[VMEM] * 3,
        out_specs=[VMEM] * len(shapes),
        out_shape=[jax.ShapeDtypeStruct(shape, jnp.float32) for shape in shapes],
        compiler_params=PARAMS,
        cost_estimate=cost(6 * rows * part * half, 4 * rows * part),
    )(*tall, panel)


def row(pair):
    return jnp.concatenate([pair[:1], pair[1:2]], axis=1)


def squares_kernel(own_ref, out_ref):
    nz, lines, _ = out_ref.shape
    part = own_ref.shape[2]
    ones = jnp.ones((lines, part), jnp.bfloat16)
    total = 0.0
    for j in range(NX):
        for piece in split(own_ref[j] * own_ref[j]):
            dims = (((1,), (1,)), ((), ()))
            total += lax.dot_general(ones, piece, dims, preferred_element_type=jnp.float32)
    for z in range(nz):
        out_ref[z] = total


def row_squares(own):
    nx, half, part = own.shape
    return pl.pallas_call(
        squares_kernel,
        in_specs=[VMEM],
        out_specs=VMEM,
        out_shape=jax.ShapeDtypeStruct((NC * NZ, 8, half), jnp.float32),
        compiler_params=PARAMS,
        cost_estimate=cost(4 * nx * half * part, 4 * nx * half * part),
    )(own)


def last_kernel(
    mine_ref, square_ref, sums_ref, m_ref, g_ref, own_ref, oth_ref,
    m_out, u_out, b_out, m_buf, u_buf, b_buf, sems,
):
    rows, (ranks, _), (half, part) = mine_ref.shape[0], b_buf.shape, own_ref.shape[1:]
    core = lax.axis_index("core")
    square = square_ref[...]
    sums = []
    for side in (core, 1 - core):
        total = sums_ref[side * NZ]
        for z in range(1, NZ):
            total = total + sums_ref[side * NZ + z]
        sums.append(total[:1])
    right_scale = jnp.sqrt(jnp.concatenate(sums, axis=0) / square + norm_eps)
    panel = mine_ref[...]
    m_left = split(panel * row((1.0 - carry_keep) / square))
    u_left = split(panel * row(math.sqrt(ROWS * COLS / RANK) / (square * right_scale)))
    left = jnp.concatenate([*m_left, *u_left], axis=0)
    left_high = jnp.concatenate([m_left[0], u_left[0]], axis=0)
    place = lax.axis_index("y") * NX + lax.axis_index("x")
    first = jnp.where(core == 0, place, NY * NX - 1 - place) * ranks
    group = pl.multiple_of(first // 8 * 8, 8)
    lane = lax.broadcasted_iota(jnp.int32, (8, half), 1)
    rank = lax.broadcasted_iota(jnp.int32, (8, half), 0) + group
    scale = 1.0 / (jnp.sqrt(square[:1]) * right_scale[:1])
    scale = jnp.sum(jnp.where(lane == rank, scale, 0.0), axis=1, keepdims=True)

    dot = functools.partial(jnp.dot, preferred_element_type=jnp.float32)
    copies = []
    for j in range(NX):
        own_at = jnp.where(core == 0, j, NX - 1 - j)
        own, columns = own_ref[own_at], pl.ds(j * part, part)
        high, low = split(jnp.concatenate([own, oth_ref[NX - 1 - own_at]], axis=0))
        sums, rest = dot(left, high), dot(left_high, low)
        feedback = sums[:rows] + sums[rows : 2 * rows] + rest[:rows]
        update = sums[2 * rows : 3 * rows] + sums[3 * rows :] + rest[rows:]
        combined = m_ref[:, columns] + g_ref[:, columns].astype(jnp.float32)
        m_buf[:, columns] = combined - feedback
        u_buf[:, columns] = update.astype(jnp.bfloat16)
        eight = own_ref[own_at, pl.ds(group, 8), :] * scale
        b_buf[:, columns] = jnp.where(first > group, eight[8 - ranks :], eight[:ranks])
        at = (slice(None), columns)
        for i, (buf, out) in enumerate(((m_buf, m_out), (u_buf, u_out))):
            copies.append(pltpu.make_async_copy(buf.at[at], out.at[at], sems.at[j, i]))
            copies[-1].start()
    copies.append(pltpu.make_async_copy(b_buf, b_out, sems.at[NX, 0]))
    copies[-1].start()
    for copy in copies:
        copy.wait()


def last_out(mine, square, sums, momentum, gradient, own, oth, ranks):
    rows, cols = momentum.shape
    half = own.shape[1]
    shapes = [
        ((rows, cols), jnp.float32),
        ((rows, cols), jnp.bfloat16),
        ((ranks, cols), jnp.float32),
    ]
    return pl.pallas_call(
        last_kernel,
        in_specs=[VMEM] * 7,
        out_specs=[HBM] * 3,
        out_shape=[jax.ShapeDtypeStruct(*shape) for shape in shapes],
        scratch_shapes=[pltpu.VMEM(*shape) for shape in shapes]
        + [pltpu.SemaphoreType.DMA((NX + 1, 2))],
        compiler_params=PARAMS,
        cost_estimate=cost(24 * rows * cols * half, 4 * (4 * rows + 2 * half) * cols),
    )(mine, square, sums, momentum, gradient, own, oth)


def exchange(blocks, axes):
    return lax.all_to_all(blocks, axes, 0, 0, tiled=True)


def turn(j):
    steps = [(x, core, (x + (j, -j)[core]) % NX) for x in range(NX) for core in range(NC)]
    return [(x * NC + core, to * NC + core) for x, core, to in steps]


def opposed(blocks, axes):
    sizes = {"y": NY, "x": NX, "core": NC, "z": NZ}
    at = np.arange(math.prod(sizes[axis] for axis in axes)).reshape([sizes[axis] for axis in axes])
    at = np.moveaxis(at, axes.index("core"), 0).reshape(NC, -1)
    groups = [at[0].tolist(), at[1, ::-1].tolist()]
    return lax.all_to_all(blocks, axes, 0, 0, axis_index_groups=groups, tiled=True)


def spread(block, axes, n):
    return opposed(jnp.broadcast_to(block[None], (n, *block.shape)), axes)


def shards(momentum, gradient, basis_panel):
    rows, cols = momentum.shape
    rank_rows = basis_panel.shape[0]
    part = cols // NX
    half = NY * NX * rank_rows
    own_ranks = NX * rank_rows
    padded = -(-rows // (8 * NZ)) * 8 * NZ

    blocks = deal(momentum + gradient.astype(jnp.float32))
    pieces = basis_pieces(basis_panel, blocks[0])
    blocks = [blocks[0]] + [
        lax.ppermute(blocks[j], ("x", "core"), turn(j)) for j in range(1, NX)
    ]
    basis_own = opposed(pieces, ("y", "x", "core"))
    basis_own, *tall = lax.optimization_barrier((basis_own, *tall_parts(blocks)))
    basis_oth = lax.ppermute(basis_own, "core", SWAP)

    panel = [panel_part(tall, basis, padded) for basis in (basis_own, basis_oth)]
    panel = jnp.concatenate(panel, axis=2)
    panel = opposed(panel.reshape(NX * NZ, padded // NZ, 2 * half), ("x", "core", "z"))
    panel = spread(jnp.sum(panel, axis=0), ("x", "core", "z"), NX * NZ)
    panel = panel.reshape(NX, padded, 2 * half)

    right_oth = lax.ppermute(right_part(1, tall, panel)[0], "core", SWAP)
    right_sum, mine = right_part(0, tall, panel)
    right_sum = right_sum + right_oth
    square = right_sum[half, : 2 * half].reshape(2, half)
    right_sum, square = lax.optimization_barrier((right_sum[:half], square))
    right_sum = opposed(right_sum.reshape(NY, own_ranks, part), ("y", "core"))
    right_sum = jnp.sum(right_sum, axis=0)
    beside = jnp.zeros((own_ranks, 128), jnp.float32).at[:2, :half].set(square)
    got = spread(jnp.concatenate([right_sum, beside], axis=1), ("y", "core"), NY)
    square = jnp.sum(got[:, :2, part : part + half], axis=0) + norm_eps

    own, square = lax.optimization_barrier((got[:, :, :part].reshape(half, part), square))
    own = spread(own, ("x", "core"), NX)
    oth = lax.ppermute(own, "core", SWAP)
    sums = exchange(row_squares(own), ("core", "z"))
    momentum_new, update, basis_new = last_out(
        mine, square, sums, momentum, gradient, own, oth, rank_rows
    )
    return momentum_new, basis_new, update


def solution(mesh):
    fine = Mesh(mesh.devices.reshape(NY, NX, NC, NZ), ("y", "x", "core", "z"))
    spec = P(("y", "x", "core"), "z")
    return jax.shard_map(
        shards,
        mesh=fine,
        in_specs=(spec, spec, spec),
        out_specs=(spec, spec, spec),
        check_vma=False,
    )
```

```python
import functools
import math

import jax
import jax.numpy as jnp
import numpy as np
from jax import lax
from jax.experimental import pallas as pl
from jax.experimental.pallas import tpu as pltpu
from jax.sharding import Mesh, PartitionSpec as P

ROWS = 7168
COLS = 28672
RANK = 256

NY, NX, NC, NZ = 8, 4, 2, 8

norm_eps = 1e-06
carry_keep = 0.9
SWAP = [(0, 1), (1, 0)]
PARAMS = pltpu.CompilerParams(vmem_limit_bytes=12 * 1024 * 1024)
VMEM = pl.BlockSpec(memory_space=pltpu.VMEM)
ANY = pl.BlockSpec(memory_space=pl.ANY)
HBM = pl.BlockSpec(memory_space=pltpu.HBM)


def split(value):
    high = value.astype(jnp.bfloat16)
    return high, (value - high.astype(jnp.float32)).astype(jnp.bfloat16)


def dot3(a, b, dims):
    dot = functools.partial(
        lax.dot_general, dimension_numbers=(dims, ((), ())), preferred_element_type=jnp.float32
    )
    return dot(a[1], b[0]) + dot(a[0], b[1]) + dot(a[0], b[0])


def cost(flops, nbytes):
    return pl.CostEstimate(flops=flops, bytes_accessed=nbytes, transcendentals=0)


def x_away(j):
    steps = jnp.where(lax.axis_index("core") == 0, j, NX - j)
    return lax.rem(lax.axis_index("x") + steps, NX)


def deal_kernel(c_ref, *blocks):
    part = blocks[0].shape[1]
    for j, ref in enumerate(blocks):
        at = x_away(j)
        ref[...] = c_ref[:, pl.ds(pl.multiple_of(at * part, 128), part)]


def deal(combined):
    rows, cols = combined.shape
    part = cols // NX
    return pl.pallas_call(
        deal_kernel,
        in_specs=[VMEM],
        out_specs=[VMEM] * NX,
        out_shape=[jax.ShapeDtypeStruct((rows, part), jnp.float32)] * NX,
        compiler_params=PARAMS,
        cost_estimate=cost(rows * cols, 8 * rows * cols),
    )(combined)


def pieces_kernel(basis_ref, after_ref, pieces_ref):
    part = pieces_ref.shape[2]
    for to in range(NX):
        at = jnp.where(lax.axis_index("core") == 0, to, NX - 1 - to)
        piece = basis_ref[:, pl.ds(pl.multiple_of(at * part, 128), part)]
        for y in range(NY):
            pieces_ref[y * NX + to] = piece


def basis_pieces(basis, after):
    ranks, cols = basis.shape
    pieces = (NY * NX, ranks, cols // NX)
    return pl.pallas_call(
        pieces_kernel,
        in_specs=[VMEM, ANY],
        out_specs=VMEM,
        out_shape=jax.ShapeDtypeStruct(pieces, jnp.float32),
        compiler_params=PARAMS,
        cost_estimate=cost(basis.size, 4 * NY * basis.size),
    )(basis, after)


def tall_kernel(*refs):
    blocks, (high_ref, low_ref) = refs[:NX], refs[NX:]
    rows = blocks[0].shape[0]
    for j, ref in enumerate(blocks):
        at = slice(j * rows, (j + 1) * rows)
        high_ref[at], low_ref[at] = split(ref[...])


def tall_parts(blocks):
    rows, part = blocks[0].shape
    shape = jax.ShapeDtypeStruct((NX * rows, part), jnp.bfloat16)
    return pl.pallas_call(
        tall_kernel,
        in_specs=[VMEM] * NX,
        out_specs=[VMEM] * 2,
        out_shape=[shape] * 2,
        compiler_params=PARAMS,
        cost_estimate=cost(10**10, 2 * 10**8),
    )(*blocks)


def panel_kernel(high_ref, low_ref, basis_ref, out_ref, buf):
    rows = high_ref.shape[0] // NX
    n, ranks, _ = basis_ref.shape
    for i in range(n):
        buf[i * ranks : (i + 1) * ranks] = basis_ref[i]
    panel = dot3((high_ref[...], low_ref[...]), split(buf[...]), ((1,), (1,)))
    for j in range(NX):
        at = x_away(NX - j)
        out_ref[at, :rows] = panel[j * rows : (j + 1) * rows]
        if out_ref.shape[1] > rows:
            spare = (out_ref.shape[1] - rows, out_ref.shape[2])
            out_ref[at, rows:] = jnp.zeros(spare, jnp.float32)


def panel_part(tall, basis, padded):
    rows, part = tall[0].shape
    half = basis.shape[0] * basis.shape[1]
    return pl.pallas_call(
        panel_kernel,
        in_specs=[VMEM] * 3,
        out_specs=VMEM,
        out_shape=jax.ShapeDtypeStruct((NX, padded, half), jnp.float32),
        scratch_shapes=[pltpu.VMEM((half, part), jnp.float32)],
        compiler_params=PARAMS,
        cost_estimate=cost(6 * rows * part * half, 4 * (rows + half) * part),
    )(*tall, basis)


def right_kernel(side, high_ref, low_ref, panel_ref, out_ref, mine_ref=None):
    rows, half = high_ref.shape[0] // NX, panel_ref.shape[2] // 2
    tall = (high_ref[...], low_ref[...])
    panel = [panel_ref[x_away(NX - j), :rows] for j in range(NX)]
    if side == 0:
        mine_ref[...] = panel[0]
    panel = jnp.concatenate(panel, axis=0)
    out_ref[half:] = jnp.zeros((8, out_ref.shape[1]), jnp.float32)
    squares = jnp.sum(panel * panel, axis=0, keepdims=True)
    out_ref[half : half + 1, :half] = squares[:, side * half : (side + 1) * half]
    out_ref[half : half + 1, half : 2 * half] = squares[:, (1 - side) * half : (2 - side) * half]
    panel = panel[:, side * half : (side + 1) * half]
    out_ref[:half] = dot3(split(panel), tall, ((0,), (0,)))


def right_part(side, tall, panel):
    rows, part = tall[0].shape
    half = panel.shape[2] // 2
    shapes = [(half + 8, part), (rows // NX, 2 * half)][: 2 - side]
    return pl.pallas_call(
        functools.partial(right_kernel, side),
        in_specs=[VMEM] * 3,
        out_specs=[VMEM] * len(shapes),
        out_shape=[jax.ShapeDtypeStruct(shape, jnp.float32) for shape in shapes],
        compiler_params=PARAMS,
        cost_estimate=cost(6 * rows * part * half, 4 * rows * part),
    )(*tall, panel)


def row(pair):
    return jnp.concatenate([pair[:1], pair[1:2]], axis=1)


def squares_kernel(own_ref, out_ref):
    nz, lines, _ = out_ref.shape
    part = own_ref.shape[2]
    ones = jnp.ones((lines, part), jnp.bfloat16)
    total = 0.0
    for j in range(NX):
        for piece in split(own_ref[j] * own_ref[j]):
            dims = (((1,), (1,)), ((), ()))
            total += lax.dot_general(ones, piece, dims, preferred_element_type=jnp.float32)
    for z in range(nz):
        out_ref[z] = total


def row_squares(own):
    nx, half, part = own.shape
    return pl.pallas_call(
        squares_kernel,
        in_specs=[VMEM],
        out_specs=VMEM,
        out_shape=jax.ShapeDtypeStruct((NC * NZ, 8, half), jnp.float32),
        compiler_params=PARAMS,
        cost_estimate=cost(4 * nx * half * part, 4 * nx * half * part),
    )(own)


def last_kernel(
    mine_ref, square_ref, sums_ref, m_ref, g_ref, own_ref, oth_ref,
    m_out, u_out, b_out, m_buf, u_buf, b_buf, sems,
):
    rows, (ranks, _), (half, part) = mine_ref.shape[0], b_buf.shape, own_ref.shape[1:]
    core = lax.axis_index("core")
    square = square_ref[...]
    sums = []
    for side in (core, 1 - core):
        total = sums_ref[side * NZ]
        for z in range(1, NZ):
            total = total + sums_ref[side * NZ + z]
        sums.append(total[:1])
    right_scale = jnp.sqrt(jnp.concatenate(sums, axis=0) / square + norm_eps)
    panel = mine_ref[...]
    m_left = split(panel * row((1.0 - carry_keep) / square))
    u_left = split(panel * row(math.sqrt(ROWS * COLS / RANK) / (square * right_scale)))
    left = jnp.concatenate([*m_left, *u_left], axis=0)
    left_high = jnp.concatenate([m_left[0], u_left[0]], axis=0)
    place = lax.axis_index("y") * NX + lax.axis_index("x")
    first = jnp.where(core == 0, place, NY * NX - 1 - place) * ranks
    group = pl.multiple_of(first // 8 * 8, 8)
    lane = lax.broadcasted_iota(jnp.int32, (8, half), 1)
    rank = lax.broadcasted_iota(jnp.int32, (8, half), 0) + group
    scale = 1.0 / (jnp.sqrt(square[:1]) * right_scale[:1])
    scale = jnp.sum(jnp.where(lane == rank, scale, 0.0), axis=1, keepdims=True)

    dot = functools.partial(jnp.dot, preferred_element_type=jnp.float32)
    copies = []
    for j in range(NX):
        own_at = jnp.where(core == 0, j, NX - 1 - j)
        own, columns = own_ref[own_at], pl.ds(j * part, part)
        high, low = split(jnp.concatenate([own, oth_ref[NX - 1 - own_at]], axis=0))
        sums, rest = dot(left, high), dot(left_high, low)
        feedback = sums[:rows] + sums[rows : 2 * rows] + rest[:rows]
        update = sums[2 * rows : 3 * rows] + sums[3 * rows :] + rest[rows:]
        combined = m_ref[:, columns] + g_ref[:, columns].astype(jnp.float32)
        m_buf[:, columns] = combined - feedback
        u_buf[:, columns] = update.astype(jnp.bfloat16)
        eight = own_ref[own_at, pl.ds(group, 8), :] * scale
        b_buf[:, columns] = jnp.where(first > group, eight[8 - ranks :], eight[:ranks])
        at = (slice(None), columns)
        for i, (buf, out) in enumerate(((m_buf, m_out), (u_buf, u_out))):
            copies.append(pltpu.make_async_copy(buf.at[at], out.at[at], sems.at[j, i]))
            copies[-1].start()
    copies.append(pltpu.make_async_copy(b_buf, b_out, sems.at[NX, 0]))
    copies[-1].start()
    for copy in copies:
        copy.wait()


def last_out(mine, square, sums, momentum, gradient, own, oth, ranks):
    rows, cols = momentum.shape
    half = own.shape[1]
    shapes = [
        ((rows, cols), jnp.float32),
        ((rows, cols), jnp.bfloat16),
        ((ranks, cols), jnp.float32),
    ]
    return pl.pallas_call(
        last_kernel,
        in_specs=[VMEM] * 7,
        out_specs=[HBM] * 3,
        out_shape=[jax.ShapeDtypeStruct(*shape) for shape in shapes],
        scratch_shapes=[pltpu.VMEM(*shape) for shape in shapes]
        + [pltpu.SemaphoreType.DMA((NX + 1, 2))],
        compiler_params=PARAMS,
        cost_estimate=cost(24 * rows * cols * half, 4 * (4 * rows + 2 * half) * cols),
    )(mine, square, sums, momentum, gradient, own, oth)


def exchange(blocks, axes):
    return lax.all_to_all(blocks, axes, 0, 0, tiled=True)


def turn(j):
    steps = [(x, core, (x + (j, -j)[core]) % NX) for x in range(NX) for core in range(NC)]
    return [(x * NC + core, to * NC + core) for x, core, to in steps]


def opposed(blocks, axes):
    sizes = {"y": NY, "x": NX, "core": NC, "z": NZ}
    at = np.arange(math.prod(sizes[axis] for axis in axes)).reshape([sizes[axis] for axis in axes])
    at = np.moveaxis(at, axes.index("core"), 0).reshape(NC, -1)
    groups = [at[0].tolist(), at[1, ::-1].tolist()]
    return lax.all_to_all(blocks, axes, 0, 0, axis_index_groups=groups, tiled=True)


def spread(block, axes, n):
    return opposed(jnp.broadcast_to(block[None], (n, *block.shape)), axes)


def shards(momentum, gradient, basis_panel):
    rows, cols = momentum.shape
    rank_rows = basis_panel.shape[0]
    part = cols // NX
    half = NY * NX * rank_rows
    own_ranks = NX * rank_rows
    padded = -(-rows // (8 * NZ)) * 8 * NZ

    blocks = deal(momentum + gradient.astype(jnp.float32))
    pieces = basis_pieces(basis_panel, blocks[0])
    blocks = [blocks[0]] + [
        lax.ppermute(blocks[j], ("x", "core"), turn(j)) for j in range(1, NX)
    ]
    basis_own = opposed(pieces, ("y", "x", "core"))
    tall = tall_parts(blocks)
    basis_oth = lax.ppermute(basis_own, "core", SWAP)

    panel = [panel_part(tall, basis, padded) for basis in (basis_own, basis_oth)]
    panel = jnp.concatenate(panel, axis=2)
    panel = opposed(panel.reshape(NX * NZ, padded // NZ, 2 * half), ("x", "core", "z"))
    panel = spread(jnp.sum(panel, axis=0), ("x", "core", "z"), NX * NZ)
    panel = panel.reshape(NX, padded, 2 * half)

    right_oth = lax.ppermute(right_part(1, tall, panel)[0], "core", SWAP)
    right_sum, mine = right_part(0, tall, panel)
    right_sum = right_sum + right_oth
    square = right_sum[half, : 2 * half].reshape(2, half)
    right_sum, square = lax.optimization_barrier((right_sum[:half], square))
    right_sum = opposed(right_sum.reshape(NY, own_ranks, part), ("y", "core"))
    right_sum = jnp.sum(right_sum, axis=0)
    beside = jnp.zeros((own_ranks, 128), jnp.float32).at[:2, :half].set(square)
    got = spread(jnp.concatenate([right_sum, beside], axis=1), ("y", "core"), NY)
    square = jnp.sum(got[:, :2, part : part + half], axis=0) + norm_eps

    own, square = lax.optimization_barrier((got[:, :, :part].reshape(half, part), square))
    own = spread(own, ("x", "core"), NX)
    oth = lax.ppermute(own, "core", SWAP)
    sums = exchange(row_squares(own), ("core", "z"))
    momentum_new, update, basis_new = last_out(
        mine, square, sums, momentum, gradient, own, oth, rank_rows
    )
    return momentum_new, basis_new, update


def solution(mesh):
    fine = Mesh(mesh.devices.reshape(NY, NX, NC, NZ), ("y", "x", "core", "z"))
    spec = P(("y", "x", "core"), "z")
    return jax.shard_map(
        shards,
        mesh=fine,
        in_specs=(spec, spec, spec),
        out_specs=(spec, spec, spec),
        check_vma=False,
    )
```

```python
import functools
import math

import jax
import jax.numpy as jnp
import numpy as np
from jax import lax
from jax.experimental import pallas as pl
from jax.experimental.pallas import tpu as pltpu
from jax.sharding import Mesh, PartitionSpec as P

ROWS = 7168
COLS = 28672
RANK = 256

NY, NX, NC, NZ = 8, 4, 2, 8

norm_eps = 1e-06
carry_keep = 0.9
SWAP = [(0, 1), (1, 0)]
PARAMS = pltpu.CompilerParams(vmem_limit_bytes=12 * 1024 * 1024)
VMEM = pl.BlockSpec(memory_space=pltpu.VMEM)
ANY = pl.BlockSpec(memory_space=pl.ANY)
HBM = pl.BlockSpec(memory_space=pltpu.HBM)


def split(value):
    high = value.astype(jnp.bfloat16)
    return high, (value - high.astype(jnp.float32)).astype(jnp.bfloat16)


def dot3(a, b, dims):
    dot = functools.partial(
        lax.dot_general, dimension_numbers=(dims, ((), ())), preferred_element_type=jnp.float32
    )
    return dot(a[1], b[0]) + dot(a[0], b[1]) + dot(a[0], b[0])


def cost(flops, nbytes):
    return pl.CostEstimate(flops=flops, bytes_accessed=nbytes, transcendentals=0)


def x_away(j):
    steps = jnp.where(lax.axis_index("core") == 0, j, NX - j)
    return lax.rem(lax.axis_index("x") + steps, NX)


def deal_kernel(c_ref, *blocks):
    part = blocks[0].shape[1]
    for j, ref in enumerate(blocks):
        at = x_away(j)
        ref[...] = c_ref[:, pl.ds(pl.multiple_of(at * part, 128), part)]


def deal(combined):
    rows, cols = combined.shape
    part = cols // NX
    return pl.pallas_call(
        deal_kernel,
        in_specs=[VMEM],
        out_specs=[VMEM] * NX,
        out_shape=[jax.ShapeDtypeStruct((rows, part), jnp.float32)] * NX,
        compiler_params=PARAMS,
        cost_estimate=cost(rows * cols, 8 * rows * cols),
    )(combined)


def pieces_kernel(basis_ref, after_ref, pieces_ref):
    part = pieces_ref.shape[2]
    for to in range(NX):
        at = jnp.where(lax.axis_index("core") == 0, to, NX - 1 - to)
        piece = basis_ref[:, pl.ds(pl.multiple_of(at * part, 128), part)]
        for y in range(NY):
            pieces_ref[y * NX + to] = piece


def basis_pieces(basis, after):
    ranks, cols = basis.shape
    pieces = (NY * NX, ranks, cols // NX)
    return pl.pallas_call(
        pieces_kernel,
        in_specs=[VMEM, ANY],
        out_specs=VMEM,
        out_shape=jax.ShapeDtypeStruct(pieces, jnp.float32),
        compiler_params=PARAMS,
        cost_estimate=cost(10**10, 10**8),
    )(basis, after)


def tall_kernel(*refs):
    blocks, (high_ref, low_ref) = refs[:NX], refs[NX:]
    rows = blocks[0].shape[0]
    for j, ref in enumerate(blocks):
        at = slice(j * rows, (j + 1) * rows)
        high_ref[at], low_ref[at] = split(ref[...])


def tall_parts(blocks):
    rows, part = blocks[0].shape
    shape = jax.ShapeDtypeStruct((NX * rows, part), jnp.bfloat16)
    return pl.pallas_call(
        tall_kernel,
        in_specs=[VMEM] * NX,
        out_specs=[VMEM] * 2,
        out_shape=[shape] * 2,
        compiler_params=PARAMS,
        cost_estimate=cost(10**10, 2 * 10**8),
    )(*blocks)


def panel_kernel(high_ref, low_ref, basis_ref, out_ref, buf):
    rows = high_ref.shape[0] // NX
    n, ranks, _ = basis_ref.shape
    for i in range(n):
        buf[i * ranks : (i + 1) * ranks] = basis_ref[i]
    panel = dot3((high_ref[...], low_ref[...]), split(buf[...]), ((1,), (1,)))
    for j in range(NX):
        at = x_away(NX - j)
        out_ref[at, :rows] = panel[j * rows : (j + 1) * rows]
        if out_ref.shape[1] > rows:
            spare = (out_ref.shape[1] - rows, out_ref.shape[2])
            out_ref[at, rows:] = jnp.zeros(spare, jnp.float32)


def panel_part(tall, basis, padded):
    rows, part = tall[0].shape
    half = basis.shape[0] * basis.shape[1]
    return pl.pallas_call(
        panel_kernel,
        in_specs=[VMEM] * 3,
        out_specs=VMEM,
        out_shape=jax.ShapeDtypeStruct((NX, padded, half), jnp.float32),
        scratch_shapes=[pltpu.VMEM((half, part), jnp.float32)],
        compiler_params=PARAMS,
        cost_estimate=cost(6 * rows * part * half, 4 * (rows + half) * part),
    )(*tall, basis)


def right_kernel(side, high_ref, low_ref, panel_ref, out_ref, mine_ref=None):
    rows, half = high_ref.shape[0] // NX, panel_ref.shape[2] // 2
    tall = (high_ref[...], low_ref[...])
    panel = [panel_ref[x_away(NX - j), :rows] for j in range(NX)]
    if side == 0:
        mine_ref[...] = panel[0]
    panel = jnp.concatenate(panel, axis=0)
    out_ref[half:] = jnp.zeros((8, out_ref.shape[1]), jnp.float32)
    squares = jnp.sum(panel * panel, axis=0, keepdims=True)
    out_ref[half : half + 1, :half] = squares[:, side * half : (side + 1) * half]
    out_ref[half : half + 1, half : 2 * half] = squares[:, (1 - side) * half : (2 - side) * half]
    panel = panel[:, side * half : (side + 1) * half]
    out_ref[:half] = dot3(split(panel), tall, ((0,), (0,)))


def right_part(side, tall, panel):
    rows, part = tall[0].shape
    half = panel.shape[2] // 2
    shapes = [(half + 8, part), (rows // NX, 2 * half)][: 2 - side]
    return pl.pallas_call(
        functools.partial(right_kernel, side),
        in_specs=[VMEM] * 3,
        out_specs=[VMEM] * len(shapes),
        out_shape=[jax.ShapeDtypeStruct(shape, jnp.float32) for shape in shapes],
        compiler_params=PARAMS,
        cost_estimate=cost(6 * rows * part * half, 4 * rows * part),
    )(*tall, panel)


def row(pair):
    return jnp.concatenate([pair[:1], pair[1:2]], axis=1)


def stack_kernel(*refs):
    for j, ref in enumerate(refs[:-1]):
        refs[-1][j] = ref[...]


def stack(blocks):
    rows, part = blocks[0].shape
    return pl.pallas_call(
        stack_kernel,
        in_specs=[VMEM] * NX,
        out_specs=VMEM,
        out_shape=jax.ShapeDtypeStruct((NX, rows, part), jnp.float32),
        compiler_params=PARAMS,
        cost_estimate=cost(NX * rows * part, 8 * NX * rows * part),
    )(*blocks)


def squares_kernel(own_ref, out_ref):
    nz, lines, _ = out_ref.shape
    part = own_ref.shape[2]
    ones = jnp.ones((lines, part), jnp.bfloat16)
    total = 0.0
    for j in range(NX):
        for piece in split(own_ref[j] * own_ref[j]):
            dims = (((1,), (1,)), ((), ()))
            total += lax.dot_general(ones, piece, dims, preferred_element_type=jnp.float32)
    for z in range(nz):
        out_ref[z] = total


def row_squares(own):
    nx, half, part = own.shape
    return pl.pallas_call(
        squares_kernel,
        in_specs=[VMEM],
        out_specs=VMEM,
        out_shape=jax.ShapeDtypeStruct((NC * NZ, 8, half), jnp.float32),
        compiler_params=PARAMS,
        cost_estimate=cost(4 * nx * half * part, 4 * nx * half * part),
    )(own)


def last_kernel(
    mine_ref, square_ref, sums_ref, m_ref, g_ref, own_ref, oth_ref,
    m_out, u_out, b_out, m_buf, u_buf, b_buf, sems,
):
    rows, (ranks, _), (half, part) = mine_ref.shape[0], b_buf.shape, own_ref.shape[1:]
    core = lax.axis_index("core")
    square = square_ref[...]
    sums = []
    for side in (core, 1 - core):
        total = sums_ref[side * NZ]
        for z in range(1, NZ):
            total = total + sums_ref[side * NZ + z]
        sums.append(total[:1])
    right_scale = jnp.sqrt(jnp.concatenate(sums, axis=0) / square + norm_eps)
    panel = mine_ref[...]
    m_left = split(panel * row((1.0 - carry_keep) / square))
    u_left = split(panel * row(math.sqrt(ROWS * COLS / RANK) / (square * right_scale)))
    left = jnp.concatenate([*m_left, *u_left], axis=0)
    left_high = jnp.concatenate([m_left[0], u_left[0]], axis=0)
    place = lax.axis_index("y") * NX + lax.axis_index("x")
    first = jnp.where(core == 0, place, NY * NX - 1 - place) * ranks
    group = pl.multiple_of(first // 8 * 8, 8)
    lane = lax.broadcasted_iota(jnp.int32, (8, half), 1)
    rank = lax.broadcasted_iota(jnp.int32, (8, half), 0) + group
    scale = 1.0 / (jnp.sqrt(square[:1]) * right_scale[:1])
    scale = jnp.sum(jnp.where(lane == rank, scale, 0.0), axis=1, keepdims=True)

    dot = functools.partial(jnp.dot, preferred_element_type=jnp.float32)
    copies = []
    for j in range(NX):
        ahead = lax.rem(NX + j - lax.axis_index("x"), NX)
        behind = lax.rem(NX - j + lax.axis_index("x"), NX)
        own_at, oth_at = jnp.where(core == 0, behind, ahead), jnp.where(core == 0, ahead, behind)
        own, columns = own_ref[own_at], pl.ds(j * part, part)
        high, low = split(jnp.concatenate([own, oth_ref[oth_at]], axis=0))
        sums, rest = dot(left, high), dot(left_high, low)
        feedback = sums[:rows] + sums[rows : 2 * rows] + rest[:rows]
        update = sums[2 * rows : 3 * rows] + sums[3 * rows :] + rest[rows:]
        combined = m_ref[:, columns] + g_ref[:, columns].astype(jnp.float32)
        m_buf[:, columns] = combined - feedback
        u_buf[:, columns] = update.astype(jnp.bfloat16)
        eight = own_ref[own_at, pl.ds(group, 8), :] * scale
        b_buf[:, columns] = jnp.where(first > group, eight[8 - ranks :], eight[:ranks])
        at = (slice(None), columns)
        for i, (buf, out) in enumerate(((m_buf, m_out), (u_buf, u_out))):
            copies.append(pltpu.make_async_copy(buf.at[at], out.at[at], sems.at[j, i]))
            copies[-1].start()
    copies.append(pltpu.make_async_copy(b_buf, b_out, sems.at[NX, 0]))
    copies[-1].start()
    for copy in copies:
        copy.wait()


def last_out(mine, square, sums, momentum, gradient, own, oth, ranks):
    rows, cols = momentum.shape
    half = own.shape[1]
    shapes = [
        ((rows, cols), jnp.float32),
        ((rows, cols), jnp.bfloat16),
        ((ranks, cols), jnp.float32),
    ]
    return pl.pallas_call(
        last_kernel,
        in_specs=[VMEM] * 7,
        out_specs=[HBM] * 3,
        out_shape=[jax.ShapeDtypeStruct(*shape) for shape in shapes],
        scratch_shapes=[pltpu.VMEM(*shape) for shape in shapes]
        + [pltpu.SemaphoreType.DMA((NX + 1, 2))],
        compiler_params=PARAMS,
        cost_estimate=cost(24 * rows * cols * half, 4 * (4 * rows + 2 * half) * cols),
    )(mine, square, sums, momentum, gradient, own, oth)


def exchange(blocks, axes):
    return lax.all_to_all(blocks, axes, 0, 0, tiled=True)


def turn(j):
    steps = [(x, core, (x + (j, -j)[core]) % NX) for x in range(NX) for core in range(NC)]
    return [(x * NC + core, to * NC + core) for x, core, to in steps]


def opposed(blocks, axes):
    sizes = {"y": NY, "x": NX, "core": NC, "z": NZ}
    at = np.arange(math.prod(sizes[axis] for axis in axes)).reshape([sizes[axis] for axis in axes])
    at = np.moveaxis(at, axes.index("core"), 0).reshape(NC, -1)
    groups = [at[0].tolist(), at[1, ::-1].tolist()]
    return lax.all_to_all(blocks, axes, 0, 0, axis_index_groups=groups, tiled=True)


def spread(block, axes, n):
    return opposed(jnp.broadcast_to(block[None], (n, *block.shape)), axes)


def shards(momentum, gradient, basis_panel):
    rows, cols = momentum.shape
    rank_rows = basis_panel.shape[0]
    part = cols // NX
    half = NY * NX * rank_rows
    own_ranks = NX * rank_rows
    padded = -(-rows // (8 * NZ)) * 8 * NZ

    blocks = deal(momentum + gradient.astype(jnp.float32))
    pieces = basis_pieces(basis_panel, blocks[0])
    blocks = [blocks[0]] + [
        lax.ppermute(blocks[j], ("x", "core"), turn(j)) for j in range(1, NX)
    ]
    basis_own = opposed(pieces, ("y", "x", "core"))
    basis_own, *tall = lax.optimization_barrier((basis_own, *tall_parts(blocks)))
    basis_oth = lax.ppermute(basis_own, "core", SWAP)

    panel = [panel_part(tall, basis, padded) for basis in (basis_own, basis_oth)]
    panel = jnp.concatenate(panel, axis=2)
    panel = opposed(panel.reshape(NX * NZ, padded // NZ, 2 * half), ("x", "core", "z"))
    panel = spread(jnp.sum(panel, axis=0), ("x", "core", "z"), NX * NZ)
    panel = panel.reshape(NX, padded, 2 * half)

    right_oth = lax.ppermute(right_part(1, tall, panel)[0], "core", SWAP)
    right_sum, mine = right_part(0, tall, panel)
    right_sum = right_sum + right_oth
    square = right_sum[half, : 2 * half].reshape(2, half)
    right_sum, square = lax.optimization_barrier((right_sum[:half], square))
    right_sum = opposed(right_sum.reshape(NY, own_ranks, part), ("y", "core"))
    right_sum = jnp.sum(right_sum, axis=0)
    beside = jnp.zeros((own_ranks, 128), jnp.float32).at[:2, :half].set(square)
    got = spread(jnp.concatenate([right_sum, beside], axis=1), ("y", "core"), NY)
    square = jnp.sum(got[:, :2, part : part + half], axis=0) + norm_eps

    own, square = lax.optimization_barrier((got[:, :, :part].reshape(half, part), square))
    own = stack([own] + [lax.ppermute(own, ("x", "core"), turn(j)) for j in range(1, NX)])
    oth = lax.ppermute(own, "core", SWAP)
    sums = exchange(row_squares(own), ("core", "z"))
    momentum_new, update, basis_new = last_out(
        mine, square, sums, momentum, gradient, own, oth, rank_rows
    )
    return momentum_new, basis_new, update


def solution(mesh):
    fine = Mesh(mesh.devices.reshape(NY, NX, NC, NZ), ("y", "x", "core", "z"))
    spec = P(("y", "x", "core"), "z")
    return jax.shard_map(
        shards,
        mesh=fine,
        in_specs=(spec, spec, spec),
        out_specs=(spec, spec, spec),
        check_vma=False,
    )
```

```python
import functools
import math

import jax
import jax.numpy as jnp
import numpy as np
from jax import lax
from jax.experimental import pallas as pl
from jax.experimental.pallas import tpu as pltpu
from jax.sharding import Mesh, PartitionSpec as P

ROWS = 7168
COLS = 28672
RANK = 256

NY, NX, NC, NZ = 8, 4, 2, 8

norm_eps = 1e-06
carry_keep = 0.9
SWAP = [(0, 1), (1, 0)]
PARAMS = pltpu.CompilerParams(vmem_limit_bytes=12 * 1024 * 1024)
VMEM = pl.BlockSpec(memory_space=pltpu.VMEM)
ANY = pl.BlockSpec(memory_space=pl.ANY)
HBM = pl.BlockSpec(memory_space=pltpu.HBM)


def split(value):
    high = value.astype(jnp.bfloat16)
    return high, (value - high.astype(jnp.float32)).astype(jnp.bfloat16)


def dot3(a, b, dims):
    dot = functools.partial(
        lax.dot_general, dimension_numbers=(dims, ((), ())), preferred_element_type=jnp.float32
    )
    return dot(a[1], b[0]) + dot(a[0], b[1]) + dot(a[0], b[0])


def cost(flops, nbytes):
    return pl.CostEstimate(flops=flops, bytes_accessed=nbytes, transcendentals=0)


def x_away(j):
    steps = jnp.where(lax.axis_index("core") == 0, j, NX - j)
    return lax.rem(lax.axis_index("x") + steps, NX)


def deal_kernel(c_ref, basis_ref, *refs):
    blocks, pieces_ref = refs[:NX], refs[NX]
    part = blocks[0].shape[1]
    for j, ref in enumerate(blocks):
        ref[...] = c_ref[:, pl.ds(pl.multiple_of(x_away(j) * part, 128), part)]
    for to in range(NX):
        at = jnp.where(lax.axis_index("core") == 0, to, NX - 1 - to)
        piece = basis_ref[:, pl.ds(pl.multiple_of(at * part, 128), part)]
        for y in range(NY):
            pieces_ref[y * NX + to] = piece


def deal(combined, basis):
    rows, cols = combined.shape
    ranks, part = basis.shape[0], cols // NX
    shapes = [(rows, part)] * NX + [(NY * NX, ranks, part)]
    return pl.pallas_call(
        deal_kernel,
        in_specs=[VMEM] * 2,
        out_specs=[VMEM] * (NX + 1),
        out_shape=[jax.ShapeDtypeStruct(shape, jnp.float32) for shape in shapes],
        compiler_params=PARAMS,
        cost_estimate=cost(rows * cols, 8 * rows * cols),
    )(combined, basis)


def tall_kernel(*refs):
    blocks, (high_ref, low_ref) = refs[:NX], refs[NX:]
    rows = blocks[0].shape[0]
    for j, ref in enumerate(blocks):
        at = slice(j * rows, (j + 1) * rows)
        high_ref[at], low_ref[at] = split(ref[...])


def tall_parts(blocks):
    rows, part = blocks[0].shape
    shape = jax.ShapeDtypeStruct((NX * rows, part), jnp.bfloat16)
    return pl.pallas_call(
        tall_kernel,
        in_specs=[VMEM] * NX,
        out_specs=[VMEM] * 2,
        out_shape=[shape] * 2,
        compiler_params=PARAMS,
        cost_estimate=cost(10**10, 2 * 10**8),
    )(*blocks)


def panel_kernel(high_ref, low_ref, basis_ref, out_ref, buf):
    rows = high_ref.shape[0] // NX
    n, ranks, _ = basis_ref.shape
    for i in range(n):
        buf[i * ranks : (i + 1) * ranks] = basis_ref[i]
    panel = dot3((high_ref[...], low_ref[...]), split(buf[...]), ((1,), (1,)))
    for j in range(NX):
        at = x_away(NX - j)
        out_ref[at, :rows] = panel[j * rows : (j + 1) * rows]
        if out_ref.shape[1] > rows:
            spare = (out_ref.shape[1] - rows, out_ref.shape[2])
            out_ref[at, rows:] = jnp.zeros(spare, jnp.float32)


def panel_part(tall, basis, padded):
    rows, part = tall[0].shape
    half = basis.shape[0] * basis.shape[1]
    return pl.pallas_call(
        panel_kernel,
        in_specs=[VMEM] * 3,
        out_specs=VMEM,
        out_shape=jax.ShapeDtypeStruct((NX, padded, half), jnp.float32),
        scratch_shapes=[pltpu.VMEM((half, part), jnp.float32)],
        compiler_params=PARAMS,
        cost_estimate=cost(6 * rows * part * half, 4 * (rows + half) * part),
    )(*tall, basis)


def right_kernel(side, high_ref, low_ref, panel_ref, out_ref, mine_ref=None):
    rows, half = high_ref.shape[0] // NX, panel_ref.shape[2] // 2
    tall = (high_ref[...], low_ref[...])
    panel = [panel_ref[x_away(NX - j), :rows] for j in range(NX)]
    if side == 0:
        mine_ref[...] = panel[0]
    panel = jnp.concatenate(panel, axis=0)
    out_ref[half:] = jnp.zeros((8, out_ref.shape[1]), jnp.float32)
    squares = jnp.sum(panel * panel, axis=0, keepdims=True)
    out_ref[half : half + 1, :half] = squares[:, side * half : (side + 1) * half]
    out_ref[half : half + 1, half : 2 * half] = squares[:, (1 - side) * half : (2 - side) * half]
    panel = panel[:, side * half : (side + 1) * half]
    out_ref[:half] = dot3(split(panel), tall, ((0,), (0,)))


def right_part(side, tall, panel):
    rows, part = tall[0].shape
    half = panel.shape[2] // 2
    shapes = [(half + 8, part), (rows // NX, 2 * half)][: 2 - side]
    return pl.pallas_call(
        functools.partial(right_kernel, side),
        in_specs=[VMEM] * 3,
        out_specs=[VMEM] * len(shapes),
        out_shape=[jax.ShapeDtypeStruct(shape, jnp.float32) for shape in shapes],
        compiler_params=PARAMS,
        cost_estimate=cost(6 * rows * part * half, 4 * rows * part),
    )(*tall, panel)


def row(pair):
    return jnp.concatenate([pair[:1], pair[1:2]], axis=1)


def squares_kernel(own_ref, out_ref):
    nz, lines, _ = out_ref.shape
    part = own_ref.shape[2]
    ones = jnp.ones((lines, part), jnp.bfloat16)
    total = 0.0
    for j in range(NX):
        for piece in split(own_ref[j] * own_ref[j]):
            dims = (((1,), (1,)), ((), ()))
            total += lax.dot_general(ones, piece, dims, preferred_element_type=jnp.float32)
    for z in range(nz):
        out_ref[z] = total


def row_squares(own):
    nx, half, part = own.shape
    return pl.pallas_call(
        squares_kernel,
        in_specs=[VMEM],
        out_specs=VMEM,
        out_shape=jax.ShapeDtypeStruct((NC * NZ, 8, half), jnp.float32),
        compiler_params=PARAMS,
        cost_estimate=cost(4 * nx * half * part, 4 * nx * half * part),
    )(own)


def last_kernel(
    mine_ref, square_ref, sums_ref, m_ref, g_ref, own_ref, oth_ref,
    m_out, u_out, b_out, m_buf, u_buf, b_buf, sems,
):
    rows, (ranks, _), (half, part) = mine_ref.shape[0], b_buf.shape, own_ref.shape[1:]
    core = lax.axis_index("core")
    square = square_ref[...]
    sums = []
    for side in (core, 1 - core):
        total = sums_ref[side * NZ]
        for z in range(1, NZ):
            total = total + sums_ref[side * NZ + z]
        sums.append(total[:1])
    right_scale = jnp.sqrt(jnp.concatenate(sums, axis=0) / square + norm_eps)
    panel = mine_ref[...]
    m_left = split(panel * row((1.0 - carry_keep) / square))
    u_left = split(panel * row(math.sqrt(ROWS * COLS / RANK) / (square * right_scale)))
    left = jnp.concatenate([*m_left, *u_left], axis=0)
    left_high = jnp.concatenate([m_left[0], u_left[0]], axis=0)
    place = lax.axis_index("y") * NX + lax.axis_index("x")
    first = jnp.where(core == 0, place, NY * NX - 1 - place) * ranks
    group = pl.multiple_of(first // 8 * 8, 8)
    lane = lax.broadcasted_iota(jnp.int32, (8, half), 1)
    rank = lax.broadcasted_iota(jnp.int32, (8, half), 0) + group
    scale = 1.0 / (jnp.sqrt(square[:1]) * right_scale[:1])
    scale = jnp.sum(jnp.where(lane == rank, scale, 0.0), axis=1, keepdims=True)

    dot = functools.partial(jnp.dot, preferred_element_type=jnp.float32)
    copies = []
    for j in range(NX):
        own_at = jnp.where(core == 0, j, NX - 1 - j)
        own, columns = own_ref[own_at], pl.ds(j * part, part)
        high, low = split(jnp.concatenate([own, oth_ref[NX - 1 - own_at]], axis=0))
        sums, rest = dot(left, high), dot(left_high, low)
        feedback = sums[:rows] + sums[rows : 2 * rows] + rest[:rows]
        update = sums[2 * rows : 3 * rows] + sums[3 * rows :] + rest[rows:]
        combined = m_ref[:, columns] + g_ref[:, columns].astype(jnp.float32)
        m_buf[:, columns] = combined - feedback
        u_buf[:, columns] = update.astype(jnp.bfloat16)
        eight = own_ref[own_at, pl.ds(group, 8), :] * scale
        b_buf[:, columns] = jnp.where(first > group, eight[8 - ranks :], eight[:ranks])
        at = (slice(None), columns)
        for i, (buf, out) in enumerate(((m_buf, m_out), (u_buf, u_out))):
            copies.append(pltpu.make_async_copy(buf.at[at], out.at[at], sems.at[j, i]))
            copies[-1].start()
    copies.append(pltpu.make_async_copy(b_buf, b_out, sems.at[NX, 0]))
    copies[-1].start()
    for copy in copies:
        copy.wait()


def last_out(mine, square, sums, momentum, gradient, own, oth, ranks):
    rows, cols = momentum.shape
    half = own.shape[1]
    shapes = [
        ((rows, cols), jnp.float32),
        ((rows, cols), jnp.bfloat16),
        ((ranks, cols), jnp.float32),
    ]
    return pl.pallas_call(
        last_kernel,
        in_specs=[VMEM] * 7,
        out_specs=[HBM] * 3,
        out_shape=[jax.ShapeDtypeStruct(*shape) for shape in shapes],
        scratch_shapes=[pltpu.VMEM(*shape) for shape in shapes]
        + [pltpu.SemaphoreType.DMA((NX + 1, 2))],
        compiler_params=PARAMS,
        cost_estimate=cost(24 * rows * cols * half, 4 * (4 * rows + 2 * half) * cols),
    )(mine, square, sums, momentum, gradient, own, oth)


def exchange(blocks, axes):
    return lax.all_to_all(blocks, axes, 0, 0, tiled=True)


def turn(j):
    steps = [(x, core, (x + (j, -j)[core]) % NX) for x in range(NX) for core in range(NC)]
    return [(x * NC + core, to * NC + core) for x, core, to in steps]


def opposed(blocks, axes):
    sizes = {"y": NY, "x": NX, "core": NC, "z": NZ}
    at = np.arange(math.prod(sizes[axis] for axis in axes)).reshape([sizes[axis] for axis in axes])
    at = np.moveaxis(at, axes.index("core"), 0).reshape(NC, -1)
    groups = [at[0].tolist(), at[1, ::-1].tolist()]
    return lax.all_to_all(blocks, axes, 0, 0, axis_index_groups=groups, tiled=True)


def spread(block, axes, n):
    return opposed(jnp.broadcast_to(block[None], (n, *block.shape)), axes)


def shards(momentum, gradient, basis_panel):
    rows, cols = momentum.shape
    rank_rows = basis_panel.shape[0]
    part = cols // NX
    half = NY * NX * rank_rows
    own_ranks = NX * rank_rows
    padded = -(-rows // (8 * NZ)) * 8 * NZ

    *blocks, pieces = deal(momentum + gradient.astype(jnp.float32), basis_panel)
    blocks = [blocks[0]] + [
        lax.ppermute(blocks[j], ("x", "core"), turn(j)) for j in range(1, NX)
    ]
    basis_own = opposed(pieces, ("y", "x", "core"))
    basis_own, *tall = lax.optimization_barrier((basis_own, *tall_parts(blocks)))
    basis_oth = lax.ppermute(basis_own, "core", SWAP)

    panel = [panel_part(tall, basis, padded) for basis in (basis_own, basis_oth)]
    panel = jnp.concatenate(panel, axis=2)
    panel = opposed(panel.reshape(NX * NZ, padded // NZ, 2 * half), ("x", "core", "z"))
    panel = spread(jnp.sum(panel, axis=0), ("x", "core", "z"), NX * NZ)
    panel = panel.reshape(NX, padded, 2 * half)

    right_oth = lax.ppermute(right_part(1, tall, panel)[0], "core", SWAP)
    right_sum, mine = right_part(0, tall, panel)
    right_sum = right_sum + right_oth
    square = right_sum[half, : 2 * half].reshape(2, half)
    right_sum, square = lax.optimization_barrier((right_sum[:half], square))
    right_sum = opposed(right_sum.reshape(NY, own_ranks, part), ("y", "core"))
    right_sum = jnp.sum(right_sum, axis=0)
    beside = jnp.zeros((own_ranks, 128), jnp.float32).at[:2, :half].set(square)
    got = spread(jnp.concatenate([right_sum, beside], axis=1), ("y", "core"), NY)
    square = jnp.sum(got[:, :2, part : part + half], axis=0) + norm_eps

    own, square = lax.optimization_barrier((got[:, :, :part].reshape(half, part), square))
    own = spread(own, ("x", "core"), NX)
    oth = lax.ppermute(own, "core", SWAP)
    sums = exchange(row_squares(own), ("core", "z"))
    momentum_new, update, basis_new = last_out(
        mine, square, sums, momentum, gradient, own, oth, rank_rows
    )
    return momentum_new, basis_new, update


def solution(mesh):
    fine = Mesh(mesh.devices.reshape(NY, NX, NC, NZ), ("y", "x", "core", "z"))
    spec = P(("y", "x", "core"), "z")
    return jax.shard_map(
        shards,
        mesh=fine,
        in_specs=(spec, spec, spec),
        out_specs=(spec, spec, spec),
        check_vma=False,
    )
```
